32 devices in a mesh: dp: 4 (over z), seq: 8 (over y, x, core).
Axes of the slice: x: 2, y: 2, z: 4, core: 2. Of those that a mesh axis runs over, the one named last changes fastest.
Arguments:
- inputs: bfloat16 [1024, 8, 1024], P('seq', 'dp'), may hold values from -6 to 6
- memory: bfloat16 [512, 8, 1024], P('seq', 'dp'), may hold values from -6 to 6
- target_length: int32 [8], P('dp'), may hold values from 768 to 1024, as said below
- memory_length: int32 [8], P('dp'), may hold values from 256 to 512, as said below
- distance_bucket: int32 [1024], replicated, may hold values from 0 to 31, as said below
- bias_table: float32 [32, 16], replicated, may hold values from -3 to 3
- self_gain: float32 [1024], replicated, may hold values from 0.5 to 1.5
- self_query: bfloat16 [1024, 1024], replicated, may hold values from -0.1875 to 0.1875
- self_key: bfloat16 [1024, 512], replicated, may hold values from -0.1875 to 0.1875
- self_value: bfloat16 [1024, 512], replicated, may hold values from -0.1875 to 0.1875
- self_out: bfloat16 [1024, 1024], replicated, may hold values from -4 to 4
- cross_gain: float32 [1024], replicated, may hold values from 0.5 to 1.5
- cross_query: bfloat16 [1024, 1024], replicated, may hold values from -0.1875 to 0.1875
- cross_key: bfloat16 [1024, 512], replicated, may hold values from -0.1875 to 0.1875
- cross_value: bfloat16 [1024, 512], replicated, may hold values from -0.1875 to 0.1875
- cross_out: bfloat16 [1024, 1024], replicated, may hold values from -3 to 3
- feed_gain: float32 [1024], replicated, may hold values from 0.5 to 1.5
- gate_weight: bfloat16 [1024, 2816], replicated, may hold values from -0.1875 to 0.1875
- up_weight: bfloat16 [1024, 2816], replicated, may hold values from -0.1875 to 0.1875
- down_weight: bfloat16 [2816, 1024], replicated, may hold values from -0.109375 to 0.109375
- upstream: bfloat16 [1024, 8, 1024], P('seq', 'dp'), may hold values from -6 to 6
Outputs:
- outputs: bfloat16 [1024, 8, 1024], P('seq', 'dp')
- input_grad: float32 [1024, 8, 1024], P('seq', 'dp')
- memory_grad: float32 [512, 8, 1024], P('seq', 'dp')
- self_gain_grad: float32 [1024], replicated
- self_query_grad: float32 [1024, 1024], P(('dp', 'seq'))
- self_key_grad: float32 [1024, 512], P(('dp', 'seq'))
- self_value_grad: float32 [1024, 512], P(('dp', 'seq'))
- self_out_grad: float32 [1024, 1024], P(('dp', 'seq'))
- bias_table_grad: float32 [32, 16], replicated
- cross_gain_grad: float32 [1024], replicated
- cross_query_grad: float32 [1024, 1024], P(('dp', 'seq'))
- cross_key_grad: float32 [1024, 512], P(('dp', 'seq'))
- cross_value_grad: float32 [1024, 512], P(('dp', 'seq'))
- cross_out_grad: float32 [1024, 1024], P(('dp', 'seq'))
- feed_gain_grad: float32 [1024], replicated
- gate_weight_grad: float32 [1024, 2816], P(('dp', 'seq'))
- up_weight_grad: float32 [1024, 2816], P(('dp', 'seq'))
- down_weight_grad: float32 [2816, 1024], P(('dp', 'seq'))
The draws below stay inside these ranges and needn't reach their ends.
Inputs may be any that keep to these rules, and one draw needn't show every extreme that they name: `target_length`: in every aligned block of 2 sequences (one index of dp) one sequence has the full length 1024 and another exactly 768. `memory_length`: in every aligned block of 2 sequences one has all 512 encoder rows and another exactly 256. `distance_bucket`: never falls with the distance; 0 at distance 0 and 31 at distance 1024 - 1.
All inputs are finite; a program needn't handle non-finite values.
Results may differ from the reference program's by a relative error of at most 0.02.
Values may be sent and summed in bfloat16 or wider, within the bound.
No kernel may reach another device: no remote copies, remote signals or barrier semaphores. Data moves between devices by JAX's collectives and lax.ppermute only.
A program may use at most 320 MiB of HBM per device.

```python
import jax
import jax.numpy as jnp
from jax import lax

D = 1024
HEADS = 16
HEAD = 64
GROUPS = 8
FF = 2816
BUCKETS = 32
MEM = 512
SEQS = 2
LEN = 1024
SEQUENCES = 8


def ragged_lengths(key, lowest, highest_len):
    first, second = jax.random.split(key)
    lengths = jax.random.randint(first, (SEQUENCES,), lowest, highest_len + 1)
    chosen = jax.random.randint(second, (SEQUENCES // SEQS,), 0, SEQS)
    slot = jnp.arange(SEQUENCES) % SEQS
    picked = jnp.repeat(chosen, SEQS, total_repeat_length=SEQUENCES)
    full = slot == picked
    short = slot == (picked + 1) % SEQS
    result = jnp.where(full, highest_len, jnp.where(short, lowest, lengths))
    return result.astype(jnp.int32)


def draw_target_length(key, part):
    key = jax.random.fold_in(key, 11)
    return ragged_lengths(key, LEN - LEN // 4, LEN)


def draw_memory_length(key, part):
    key = jax.random.fold_in(key, 12)
    return ragged_lengths(key, MEM // 2, MEM)


def draw_distance_bucket(key, part):
    key = jax.random.fold_in(key, 13)
    places = jnp.arange(LEN)
    steps = jax.random.randint(key, (LEN,), 0, 2)
    steps = jnp.where(places == 0, 0, steps)
    climb = jnp.minimum(jnp.cumsum(steps), BUCKETS - 1)
    return jnp.where(places == LEN - 1, BUCKETS - 1, climb).astype(jnp.int32)


def block_scale(rng, dims, cuts, low, high):
    factor_of = 1.0
    for dim, blocks in cuts:
        draws = jax.random.uniform(jax.random.fold_in(jax.random.fold_in(rng, 6), dim), (blocks,), jnp.float32, low / len(cuts), high / len(cuts))
        factor_of = factor_of * jnp.repeat(jnp.exp(draws), dims[dim] // blocks).reshape((-1,) + (1,) * (len(dims) - 1 - dim))
    return factor_of


def gaussian(key, shape, deviation, limit, pieces=(), held_as=jnp.bfloat16):
    entries = deviation * jax.random.normal(key, shape, jnp.float32)
    if pieces:
        entries = entries * block_scale(key, shape, pieces, -0.22, 0.18)
    return jnp.clip(entries, -limit, limit).astype(held_as)


def setup_inputs(seed: int = 0) -> dict:
    key_of = jax.random.split(jax.random.key(seed), 22)
    inputs = gaussian(key_of[0], (LEN, SEQUENCES, D), 1.0, 6.0, ((0, 8), (1, 4)))
    memory = gaussian(key_of[1], (MEM, SEQUENCES, D), 1.0, 6.0, ((0, 8), (1, 4)))
    target_length = draw_target_length(jax.random.fold_in(key_of[21], 71), 0)
    memory_length = draw_memory_length(jax.random.fold_in(key_of[21], 71), 0)
    distance_bucket = draw_distance_bucket(jax.random.fold_in(key_of[21], 71), 0)
    bias_table = gaussian(key_of[5], (BUCKETS, HEADS), 0.5, 3.0, (), jnp.float32)
    self_gain = jnp.clip(1.0 + 0.1 * jax.random.normal(key_of[6], (D,), jnp.float32), 0.5, 1.5)
    self_query = gaussian(key_of[7], (D, HEADS * HEAD), D ** -0.5, 0.1875)
    self_key = gaussian(key_of[8], (D, GROUPS * HEAD), D ** -0.5, 0.1875)
    self_value = gaussian(key_of[9], (D, GROUPS * HEAD), D ** -0.5, 0.1875)
    self_out = gaussian(key_of[10], (HEADS * HEAD, D), (max(1, 2 * D // LEN)) ** -0.5, 4.0)
    cross_gain = jnp.clip(1.0 + 0.1 * jax.random.normal(key_of[11], (D,), jnp.float32), 0.5, 1.5)
    cross_query = gaussian(key_of[12], (D, HEADS * HEAD), D ** -0.5, 0.1875)
    cross_key = gaussian(key_of[13], (D, GROUPS * HEAD), D ** -0.5, 0.1875)
    cross_value = gaussian(key_of[14], (D, GROUPS * HEAD), D ** -0.5, 0.1875)
    cross_out = gaussian(key_of[15], (HEADS * HEAD, D), (max(1, 2 * D // MEM)) ** -0.5, 3.0)
    feed_gain = jnp.clip(1.0 + 0.1 * jax.random.normal(key_of[16], (D,), jnp.float32), 0.5, 1.5)
    gate_weight = gaussian(key_of[17], (D, FF), D ** -0.5, 0.1875)
    up_weight = gaussian(key_of[18], (D, FF), D ** -0.5, 0.1875)
    down_weight = gaussian(key_of[19], (FF, D), FF ** -0.5, 0.109375)
    upstream = gaussian(key_of[20], (LEN, SEQUENCES, D), 1.0, 6.0, ((0, 8), (1, 4)))
    return dict(inputs=inputs, memory=memory, target_length=target_length, memory_length=memory_length, distance_bucket=distance_bucket, bias_table=bias_table, self_gain=self_gain, self_query=self_query, self_key=self_key, self_value=self_value, self_out=self_out, cross_gain=cross_gain, cross_query=cross_query, cross_key=cross_key, cross_value=cross_value, cross_out=cross_out, feed_gain=feed_gain, gate_weight=gate_weight, up_weight=up_weight, down_weight=down_weight, upstream=upstream)


@jax.custom_vjp
def low(v):
    return lax.optimization_barrier(v.astype(jnp.bfloat16)).astype(jnp.float32)

@jax.custom_vjp
def low_back(v):
    return v

def low_keep(v):
    return (low(v), None)

def low_pass(kept, grad):
    return (grad,)

def back_keep(v):
    return (v, None)

def back_low(kept, grad):
    return (low(grad),)
low.defvjp(low_keep, low_pass)
low_back.defvjp(back_keep, back_low)
epsilon = 1e-06
scale = 0.125
highest = lax.Precision.HIGHEST

def product(left, right):
    return jnp.dot(left, right, precision=highest)

def rms_norm(value, gain):
    return value * lax.rsqrt(lax.optimization_barrier(jnp.mean(value * value, axis=-1, keepdims=True)) + epsilon) * gain

def attention(query, keys, values, extra, allowed):
    rows = query.shape[0]
    count = keys.shape[0]
    heads = query.reshape(rows, GROUPS, HEADS // GROUPS, HEAD)
    keyset = keys.reshape(count, GROUPS, HEAD)
    valset = values.reshape(count, GROUPS, HEAD)
    scores = scale * jnp.einsum('tgrd,lgd->grtl', heads, keyset, precision=highest) + extra
    scores = low_back(scores)
    scores = jnp.where(allowed, scores, -1e+30)
    shares = low(jax.nn.softmax(scores, axis=-1))
    mixed = jnp.einsum('grtl,lgd->tgrd', shares, valset, precision=highest)
    return mixed.reshape(rows, HEADS * HEAD)

def layer(params, inputs, memory, target, memlen, distance_bucket):
    self_gain, self_query, self_key, self_value, self_out, bias_table, cross_gain, cross_query, cross_key, cross_value, cross_out, feed_gain, gate_weight, up_weight, down_weight = params
    length = inputs.shape[0]
    positions = jnp.arange(length)
    normed = low(rms_norm(inputs, self_gain))
    query = low_back(low(product(normed, self_query)))
    keys = low_back(low(product(normed, self_key)))
    values = low_back(low(product(normed, self_value)))
    offset = jnp.clip(positions[:, None] - positions[None, :], 0, length - 1)
    extra = jnp.transpose(bias_table[distance_bucket][offset], (2, 0, 1))
    extra = extra.reshape(GROUPS, HEADS // GROUPS, length, length)
    allowed = (positions[None, :] <= positions[:, None]) & (positions[None, :] < target)
    mixed = low_back(low(attention(query, keys, values, extra, allowed)))
    first = inputs + low_back(product(mixed, self_out))
    normed = low(rms_norm(first, cross_gain))
    recall_query = low_back(low(product(normed, cross_query)))
    recall_keys = low_back(low(product(memory, cross_key)))
    recall_values = low_back(low(product(memory, cross_value)))
    rows = memory.shape[0]
    recall_allowed = jnp.broadcast_to(jnp.arange(rows)[None, :] < memlen, (length, rows))
    recall_mixed = low_back(low(attention(recall_query, recall_keys, recall_values, 0.0, recall_allowed)))
    second = first + low_back(product(recall_mixed, cross_out))
    normed = low(rms_norm(second, feed_gain))
    gate = low_back(product(normed, gate_weight))
    upper = low_back(product(normed, up_weight))
    hidden = low(jax.nn.gelu(gate, approximate=True) * upper)
    result = second + low_back(product(hidden, down_weight))
    return jnp.where((positions < target)[:, None], result, 0.0)

def reference(inputs, memory, target_length, memory_length, distance_bucket, bias_table, self_gain, self_query, self_key, self_value, self_out, cross_gain, cross_query, cross_key, cross_value, cross_out, feed_gain, gate_weight, up_weight, down_weight, upstream):
    params = tuple((weight.astype(jnp.float32) for weight in (self_gain, self_query, self_key, self_value, self_out, bias_table, cross_gain, cross_query, cross_key, cross_value, cross_out, feed_gain, gate_weight, up_weight, down_weight)))

    def whole(params, inputs, memory):

        def single(pack):
            return layer(params, pack[0], pack[1], pack[2], pack[3], distance_bucket)
        return lax.map(jax.checkpoint(single), (jnp.moveaxis(inputs, 1, 0), jnp.moveaxis(memory, 1, 0), target_length, memory_length))
    result, backward = jax.vjp(whole, params, inputs.astype(jnp.float32), memory.astype(jnp.float32))
    grads, input_grad, memory_grad = backward(jnp.moveaxis(upstream.astype(jnp.float32), 1, 0))
    outputs = jnp.moveaxis(result, 0, 1).astype(jnp.bfloat16)
    return (outputs, input_grad, memory_grad, grads[0], grads[1], grads[2], grads[3], grads[4], grads[5], grads[6], grads[7], grads[8], grads[9], grads[10], grads[11], grads[12], grads[13], grads[14])
```

```python
import jax
import jax.numpy as jnp
from jax import lax
from jax.experimental import pallas as pl
from jax.sharding import PartitionSpec as P

GROUPS = 8


epsilon = 1e-06
scale = 0.125
negative = -1e30
highest = lax.Precision.HIGHEST


def copy_kernel(a_ref, b_ref):
    b_ref[...] = a_ref[...]


def rms_norm(value, gain):
    return value * lax.rsqrt(jnp.mean(value * value, axis=-1, keepdims=True) + epsilon) * gain


def gating(gate, upper):
    return jax.nn.gelu(gate, approximate=True) * upper


def project(left, right):
    return jnp.einsum("tsd,de->tse", left, right, preferred_element_type=jnp.float32)


def weight_grad(left, right):
    return jnp.einsum("tsd,tse->de", left, right, preferred_element_type=jnp.float32)


def back_project(grad, right):
    return jnp.einsum("tse,de->tsd", grad, right, preferred_element_type=jnp.float32)


def pick(array, index):
    return lax.dynamic_index_in_dim(array, index, 1, keepdims=False)


def place(array, piece, index):
    return lax.dynamic_update_index_in_dim(array, piece, index, 1)


def split_heads(query, keys):
    width = keys.shape[1] // GROUPS
    heads = query.reshape(query.shape[0], GROUPS, -1, width)
    return (heads, keys.reshape(keys.shape[0], GROUPS, width))


def raw_scores(heads, keyset, extra, allowed):
    scores = scale * jnp.einsum("tgrd,lgd->grtl", heads, keyset, preferred_element_type=jnp.float32)
    if extra is not None:
        scores = scores + extra
    return jnp.where(allowed, scores, negative)


def attend(query, keys, values, extra, allowed):
    heads, keyset = split_heads(query, keys)
    valset = values.reshape(keyset.shape)
    scores = raw_scores(heads, keyset, extra, allowed)
    peak = jnp.max(scores, axis=-1, keepdims=True)
    raised = jnp.exp(scores - peak)
    total = jnp.sum(raised, axis=-1, keepdims=True)
    shares = (raised / total).astype(jnp.bfloat16)
    mixed = jnp.einsum("grtl,lgd->tgrd", shares, valset, preferred_element_type=jnp.float32)
    return (mixed.reshape(query.shape).astype(jnp.bfloat16), (peak + jnp.log(total))[..., 0])


def attend_back(query, keys, values, extra, allowed, logsum, upstream):
    heads, keyset = split_heads(query, keys)
    valset = values.reshape(keyset.shape)
    scores = raw_scores(heads, keyset, extra, allowed)
    shares = jnp.exp(scores - logsum[..., None])
    incoming = upstream.reshape(heads.shape)
    share_grad = jnp.einsum("tgrd,lgd->grtl", incoming, valset, preferred_element_type=jnp.float32)
    inner = jnp.sum(shares * share_grad, axis=-1, keepdims=True)
    score_grad = (shares * (share_grad - inner)).astype(jnp.bfloat16)
    query_grad = scale * jnp.einsum(
        "grtl,lgd->tgrd", score_grad, keyset, preferred_element_type=jnp.float32
    )
    key_grad = scale * jnp.einsum(
        "grtl,tgrd->lgd", score_grad, heads, preferred_element_type=jnp.float32
    )
    value_grad = jnp.einsum(
        "grtl,tgrd->lgd", shares.astype(jnp.bfloat16), incoming, preferred_element_type=jnp.float32
    )
    return (
        query_grad.reshape(query.shape).astype(jnp.bfloat16),
        key_grad.reshape(keys.shape),
        value_grad.reshape(keys.shape),
        score_grad,
    )


def per_device(
    inputs,
    memory,
    target_length,
    memory_length,
    distance_bucket,
    bias_table,
    self_gain,
    self_query,
    self_key,
    self_value,
    self_out,
    cross_gain,
    cross_query,
    cross_key,
    cross_value,
    cross_out,
    feed_gain,
    gate_weight,
    up_weight,
    down_weight,
    upstream,
):
    tokens, seqs, width = inputs.shape
    length = tokens * lax.axis_size("seq")
    buckets = bias_table.shape[0]
    head_cols = self_query.shape[1]
    group_cols = self_key.shape[1]
    hidden_cols = gate_weight.shape[1]
    positions = lax.axis_index("seq") * tokens + jnp.arange(tokens, dtype=jnp.int32)
    columns = jnp.arange(length, dtype=jnp.int32)
    live = positions[:, None] < target_length[None, :]
    causal = columns[None, :] <= positions[:, None]
    offset = jnp.clip(positions[:, None] - columns[None, :], 0, length - 1)
    bucket_ids = jnp.arange(buckets, dtype=jnp.int32)
    thresholds = jnp.sum((distance_bucket[None, :] < bucket_ids[:, None]).astype(jnp.int32), axis=1)
    pair_bucket = jnp.sum(
        (offset[None, :, :] >= thresholds[1:, None, None]).astype(jnp.int32), axis=0
    )
    bucket_match = bucket_ids[:, None, None] == pair_bucket[None, :, :]
    extra = jnp.einsum(
        "btl,bh->htl", bucket_match.astype(jnp.float32), bias_table, precision=highest
    ).reshape(GROUPS, -1, tokens, length)
    bucket_onehot = bucket_match.astype(jnp.bfloat16)
    inputs_float = inputs.astype(jnp.float32)
    normed_self = rms_norm(inputs_float, self_gain).astype(jnp.bfloat16)
    query = project(normed_self, self_query).astype(jnp.bfloat16)
    keys = project(normed_self, self_key).astype(jnp.bfloat16)
    values = project(normed_self, self_value).astype(jnp.bfloat16)
    all_keys, all_values = (
        lax.all_gather(keys, "seq", axis=0, tiled=True),
        lax.all_gather(values, "seq", axis=0, tiled=True),
    )
    memory_keys = project(memory, cross_key).astype(jnp.bfloat16)
    memory_values = project(memory, cross_value).astype(jnp.bfloat16)
    recall_keys, recall_values = (
        lax.all_gather(memory_keys, "seq", axis=0, tiled=True),
        lax.all_gather(memory_values, "seq", axis=0, tiled=True),
    )
    mem_rows = recall_keys.shape[0]
    reach = jnp.arange(mem_rows, dtype=jnp.int32)

    def self_allowed(index):
        return causal & (columns[None, :] < target_length[index])

    def cross_allowed(index):
        return jnp.broadcast_to(reach[None, :] < memory_length[index], (tokens, mem_rows))

    def self_forward(index, carry):
        mixed_all, logsum_all = carry
        mixed, logsum = attend(
            pick(query, index),
            pick(all_keys, index),
            pick(all_values, index),
            extra,
            self_allowed(index),
        )
        return (
            place(mixed_all, mixed, index),
            lax.dynamic_update_index_in_dim(logsum_all, logsum, index, 0),
        )

    self_mixed, self_logsum = lax.fori_loop(
        0,
        seqs,
        self_forward,
        (jnp.zeros(query.shape, jnp.bfloat16), jnp.zeros((seqs,) + extra.shape[:3], jnp.float32)),
    )
    first = inputs_float + project(self_mixed, self_out)
    normed_cross = rms_norm(first, cross_gain).astype(jnp.bfloat16)
    recall_query = project(normed_cross, cross_query).astype(jnp.bfloat16)

    def cross_forward(index, carry):
        mixed_all, logsum_all = carry
        mixed, logsum = attend(
            pick(recall_query, index),
            pick(recall_keys, index),
            pick(recall_values, index),
            None,
            cross_allowed(index),
        )
        return (
            place(mixed_all, mixed, index),
            lax.dynamic_update_index_in_dim(logsum_all, logsum, index, 0),
        )

    cross_mixed, cross_logsum = lax.fori_loop(
        0,
        seqs,
        cross_forward,
        (
            jnp.zeros(recall_query.shape, jnp.bfloat16),
            jnp.zeros((seqs,) + extra.shape[:3], jnp.float32),
        ),
    )
    second = first + project(cross_mixed, cross_out)
    normed_feed = rms_norm(second, feed_gain).astype(jnp.bfloat16)
    gate = project(normed_feed, gate_weight)
    upper = project(normed_feed, up_weight)
    hidden = gating(gate, upper).astype(jnp.bfloat16)
    result = second + project(hidden, down_weight)
    outputs = jnp.where(live[..., None], result, 0.0).astype(jnp.bfloat16)
    grad = jnp.where(live[..., None], upstream.astype(jnp.float32), 0.0)
    grad_low = grad.astype(jnp.bfloat16)
    down_grad = weight_grad(hidden, grad_low)
    hidden_grad = back_project(grad_low, down_weight)
    unused, gate_back = jax.vjp(gating, gate, upper)
    gate_grad, upper_grad = gate_back(hidden_grad)
    gate_grad = gate_grad.astype(jnp.bfloat16)
    upper_grad = upper_grad.astype(jnp.bfloat16)
    feed_weights_grad = weight_grad(normed_feed, jnp.concatenate([gate_grad, upper_grad], axis=-1))
    feed_in = back_project(gate_grad, gate_weight) + back_project(upper_grad, up_weight)
    unused, norm_back = jax.vjp(rms_norm, second, feed_gain)
    second_part, feed_gain_grad = norm_back(feed_in)
    second_grad = grad + second_part
    second_low = second_grad.astype(jnp.bfloat16)
    cross_out_grad = weight_grad(cross_mixed, second_low)
    cross_mixed_grad = back_project(second_low, cross_out).astype(jnp.bfloat16)

    def cross_backward(index, carry):
        query_all, key_all, value_all = carry
        query_grad, key_grad, value_grad, score_grad = attend_back(
            pick(recall_query, index),
            pick(recall_keys, index),
            pick(recall_values, index),
            None,
            cross_allowed(index),
            cross_logsum[index],
            pick(cross_mixed_grad, index),
        )
        return (
            place(query_all, query_grad, index),
            place(key_all, key_grad, index),
            place(value_all, value_grad, index),
        )

    recall_query_grad, recall_key_part, recall_value_part = lax.fori_loop(
        0,
        seqs,
        cross_backward,
        (
            jnp.zeros(recall_query.shape, jnp.bfloat16),
            jnp.zeros(recall_keys.shape, jnp.float32),
            jnp.zeros(recall_keys.shape, jnp.float32),
        ),
    )
    memory_key_grad, memory_value_grad = (
        lax.psum_scatter(
            recall_key_part.astype(jnp.bfloat16), "seq", scatter_dimension=0, tiled=True
        ).astype(jnp.float32),
        lax.psum_scatter(
            recall_value_part.astype(jnp.bfloat16), "seq", scatter_dimension=0, tiled=True
        ).astype(jnp.float32),
    )
    memory_key_low = memory_key_grad.astype(jnp.bfloat16)
    memory_value_low = memory_value_grad.astype(jnp.bfloat16)
    cross_kv_weights_grad = weight_grad(
        memory, jnp.concatenate([memory_key_low, memory_value_low], axis=-1)
    )
    memory_grad = back_project(memory_key_low, cross_key) + back_project(
        memory_value_low, cross_value
    )
    cross_query_grad = weight_grad(normed_cross, recall_query_grad)
    cross_in = back_project(recall_query_grad, cross_query)
    unused, norm_back = jax.vjp(rms_norm, first, cross_gain)
    first_part, cross_gain_grad = norm_back(cross_in)
    first_grad = second_grad + first_part
    first_low = first_grad.astype(jnp.bfloat16)
    self_out_grad = weight_grad(self_mixed, first_low)
    self_mixed_grad = back_project(first_low, self_out).astype(jnp.bfloat16)
    used_keys, used_values = (all_keys, all_values)

    def self_backward(index, carry):
        query_all, key_all, value_all, table_all = carry
        query_grad, key_grad, value_grad, score_grad = attend_back(
            pick(query, index),
            pick(used_keys, index),
            pick(used_values, index),
            extra,
            self_allowed(index),
            self_logsum[index],
            pick(self_mixed_grad, index),
        )
        table_all = table_all + jnp.einsum(
            "grtl,btl->grb", score_grad, bucket_onehot, preferred_element_type=jnp.float32
        )
        return (
            place(query_all, query_grad, index),
            place(key_all, key_grad, index),
            place(value_all, value_grad, index),
            table_all,
        )

    query_grad_all, key_part, value_part, table_all = lax.fori_loop(
        0,
        seqs,
        self_backward,
        (
            jnp.zeros(query.shape, jnp.bfloat16),
            jnp.zeros(used_keys.shape, jnp.float32),
            jnp.zeros(used_keys.shape, jnp.float32),
            jnp.zeros(extra.shape[:2] + (buckets,), jnp.float32),
        ),
    )
    key_local, value_local = (
        lax.psum_scatter(
            key_part.astype(jnp.bfloat16), "seq", scatter_dimension=0, tiled=True
        ).astype(jnp.float32),
        lax.psum_scatter(
            value_part.astype(jnp.bfloat16), "seq", scatter_dimension=0, tiled=True
        ).astype(jnp.float32),
    )
    key_low = key_local.astype(jnp.bfloat16)
    value_low = value_local.astype(jnp.bfloat16)
    self_weights_grad = weight_grad(
        normed_self, jnp.concatenate([query_grad_all, key_low, value_low], axis=-1)
    )
    self_in = (
        back_project(query_grad_all, self_query)
        + back_project(key_low, self_key)
        + back_project(value_low, self_value)
    )
    unused, norm_back = jax.vjp(rms_norm, inputs_float, self_gain)
    input_part, self_gain_grad = norm_back(self_in)
    input_grad = first_grad + input_part
    table_grad = table_all.reshape(-1, buckets).T
    table_grad = pl.pallas_call(copy_kernel, out_shape=jax.ShapeDtypeStruct(table_grad.shape, jnp.float32))(table_grad)
    gains = jnp.concatenate([self_gain_grad, cross_gain_grad, feed_gain_grad])
    gain_sum, table_sum = lax.psum((gains, table_grad), ("dp", "seq"))
    rows_block = jnp.concatenate(
        [self_weights_grad, cross_query_grad, cross_kv_weights_grad, feed_weights_grad], axis=1
    )
    out_block = jnp.concatenate([self_out_grad, cross_out_grad], axis=1)
    rows_part, out_part, down_part = (
        lax.psum_scatter(rows_block, ("dp", "seq"), scatter_dimension=0, tiled=True),
        lax.psum_scatter(out_block, ("dp", "seq"), scatter_dimension=0, tiled=True),
        lax.psum_scatter(down_grad, ("dp", "seq"), scatter_dimension=0, tiled=True),
    )
    cuts = [
        head_cols,
        group_cols,
        group_cols,
        head_cols,
        group_cols,
        group_cols,
        hidden_cols,
        hidden_cols,
    ]
    pieces = []
    start = 0
    for cut in cuts:
        pieces.append(rows_part[:, start : start + cut])
        start = start + cut
    return (
        outputs,
        input_grad,
        memory_grad,
        gain_sum[:width],
        pieces[0],
        pieces[1],
        pieces[2],
        out_part[:, :width],
        table_sum,
        gain_sum[width : 2 * width],
        pieces[3],
        pieces[4],
        pieces[5],
        out_part[:, width:],
        gain_sum[2 * width :],
        pieces[6],
        pieces[7],
        down_part,
    )


def solution(mesh):
    placed = (
        P("seq", "dp", None),
        P("seq", "dp", None),
        P("dp"),
        P("dp"),
        P(),
        P(),
        P(),
        P(),
        P(),
        P(),
        P(),
        P(),
        P(),
        P(),
        P(),
        P(),
        P(),
        P(),
        P(),
        P(),
        P("seq", "dp", None),
    )
    return jax.shard_map(
        per_device,
        mesh=mesh,
        in_specs=placed,
        out_specs=(
            P("seq", "dp", None),
            P("seq", "dp", None),
            P("seq", "dp", None),
            P(),
            P(("dp", "seq"), None),
            P(("dp", "seq"), None),
            P(("dp", "seq"), None),
            P(("dp", "seq"), None),
            P(),
            P(),
            P(("dp", "seq"), None),
            P(("dp", "seq"), None),
            P(("dp", "seq"), None),
            P(("dp", "seq"), None),
            P(),
            P(("dp", "seq"), None),
            P(("dp", "seq"), None),
            P(("dp", "seq"), None),
        ),
        check_vma=False,
    )
```

```python
import functools

import jax
import jax.numpy as jnp
from jax import lax
from jax.experimental import pallas as pl
from jax.experimental.pallas import tpu as pltpu
from jax.sharding import PartitionSpec as P

GROUPS = 8


epsilon = 1e-06
scale = 0.125
negative = -1e30
highest = lax.Precision.HIGHEST
bf16 = jnp.bfloat16
f32 = jnp.float32


def norm_rate(value):
    return lax.rsqrt(jnp.mean(value * value, axis=-1, keepdims=True) + epsilon)


def norm_back(value, rate, gain, incoming):
    scaled = incoming * gain
    inner = jnp.mean(scaled * value, axis=-1, keepdims=True)
    grad = rate * (scaled - value * (rate * rate * inner))
    return grad, jnp.sum(incoming * value * rate, axis=0)


def mm(left, right):
    return jnp.dot(left, right, preferred_element_type=f32)


def mm_t(grad, weight):
    return lax.dot_general(grad, weight, (((1,), (1,)), ((), ())), preferred_element_type=f32)


def exchange(value, axis, bit):
    size = lax.axis_size(axis)
    return lax.ppermute(value, axis, [(i, i ^ bit) for i in range(size)])


def bits_of(size, lowest):
    bits = []
    bit = lowest
    while bit < size:
        bits.append(bit)
        bit = bit * 2
    return bits


TILE = 256


def grad_order(flip):
    seq_bits = bits_of(lax.axis_size("seq"), 2)
    if flip:
        seq_bits = seq_bits[::-1]
    return [("seq", b) for b in seq_bits] + [("dp", b) for b in bits_of(lax.axis_size("dp"), 1)]


def grads_kernel(chips, orders, tasks, sources, count, me_ref, *refs):
    ins, refs = refs[:sources], refs[count:]
    outs, (turned, total) = refs[:4], refs[4:]
    blocks = 2 ** len(orders[0])
    filled = [0, 0]
    for (xo, xp, do, dp), tokens, rows, rchip, tiles in tasks:
        for half, (place, lane) in enumerate((xo, xp)):
            turned[:rows, half * tokens : (half + 1) * tokens] = ins[place][:, lane : lane + rows].T
        for stack, lane in tiles:
            value = mm(turned[:rows, :tokens], ins[do[0]][:, do[1] + lane : do[1] + lane + TILE])
            value = value + mm(
                turned[:rows, tokens : 2 * tokens], ins[dp[0]][:, dp[1] + lane : dp[1] + lane + TILE]
            )
            for block in range(blocks):
                total[block, :rchip] = value[block * rchip : (block + 1) * rchip]
            order = orders[stack]
            for slot in range(blocks):
                seq_part, dp_part = 0, 0
                for place, (axis, bit) in enumerate(order):
                    if (slot >> (len(order) - 1 - place)) & 1:
                        if axis == "seq":
                            seq_part = seq_part | (bit // 2)
                        else:
                            dp_part = dp_part | bit
                block = (me_ref[0] ^ dp_part) * chips + (me_ref[1] ^ seq_part)
                outs[2 * stack + slot // (blocks // 2)][
                    slot % (blocks // 2), filled[stack] : filled[stack] + rchip
                ] = total[block, :rchip].astype(bf16)
            filled[stack] += rchip


def group_grads(arrays, tasks, after=()):
    chips = lax.axis_size("seq") // 2
    orders = [grad_order(False), grad_order(True)]
    blocks = 2 ** len(orders[0])
    full = []
    depth = [0, 0]
    flops = 0
    for names, rows, tiles in tasks:
        tokens = arrays[names[0][0]].shape[0]
        full.append((names, tokens, rows, rows // blocks, tiles))
        flops += 4 * tokens * rows * TILE * len(tiles)
        for stack, lane in tiles:
            depth[stack] += rows // blocks
    me = jnp.stack([lax.axis_index("dp"), lax.axis_index("seq") // 2]).astype(jnp.int32)
    vmem = pl.BlockSpec(memory_space=pltpu.VMEM)
    most = max(t[2] for t in full)
    shapes = [jax.ShapeDtypeStruct((blocks // 2, depth[i // 2], TILE), bf16) for i in range(4)]
    total = arrays[0].dtype.itemsize * sum(a.size for a in arrays)
    return pl.pallas_call(
        functools.partial(grads_kernel, chips, orders, full, len(arrays), len(arrays) + len(after)),
        in_specs=[pl.BlockSpec(memory_space=pltpu.SMEM)]
        + [vmem] * len(arrays)
        + [pl.BlockSpec(memory_space=pl.ANY)] * len(after),
        out_specs=[vmem] * 4,
        scratch_shapes=[
            pltpu.VMEM((most, max(2 * t[1] for t in full)), bf16),
            pltpu.VMEM((blocks, most // blocks, TILE), f32),
        ],
        out_shape=shapes,
        compiler_params=pltpu.CompilerParams(vmem_limit_bytes=44 * 1024 * 1024),
        cost_estimate=pl.CostEstimate(
            flops=flops, bytes_accessed=total + 4 * sum(depth) * blocks * TILE, transcendentals=0
        ),
    )(me, *arrays, *after)


class Chain:
    def __init__(self, outs):
        self.keep, self.send = [outs[0], outs[2]], [outs[1], outs[3]]
        self.orders = [grad_order(False), grad_order(True)]
        self.level = 0
        self.joint = False

    def step(self):
        order = self.orders[0]
        joint = order[self.level][0] == "dp"
        if joint and not self.joint:
            self.keep = [jnp.concatenate(self.keep, axis=1)]
            self.send = [jnp.concatenate(self.send, axis=1)]
            self.joint = True
        got = [
            exchange(v, *self.orders[i][self.level]) for i, v in enumerate(self.send)
        ]
        self.level += 1
        half = got[0].shape[0] // 2
        if half:
            self.send = [k[half:] + g[half:] for k, g in zip(self.keep, got)]
            self.keep = [k[:half] + g[:half] for k, g in zip(self.keep, got)]
        else:
            self.keep = [k.astype(f32) + g.astype(f32) for k, g in zip(self.keep, got)]
        return got

    def finish(self):
        while self.level < len(self.orders[0]):
            self.step()
        return self.keep[0][0]


def swap_rows(parts):
    lows, highs = [], []
    for part in parts:
        half = part.shape[1] // 2
        lows.append(part[:, :half].reshape(-1, TILE))
        highs.append(part[:, half:].reshape(-1, TILE))
    low = jnp.concatenate(lows, axis=0)
    high = jnp.concatenate(highs, axis=0)
    mine, other = core_halves(low, high)
    got = exchange(other.astype(bf16), "seq", 1).astype(f32)
    first, second = core_halves(mine, got)
    done = []
    start = 0
    for part in parts:
        tiles, half = part.shape[0], part.shape[1] // 2
        pair = []
        for whole in (first, second):
            piece = whole[start : start + tiles * half].reshape(tiles, half, TILE)
            pair.append(jnp.transpose(piece, (1, 0, 2)).reshape(half, tiles * TILE))
        done.append(tuple(pair))
        start += tiles * half
    return done


def core_halves(left, right):
    core = lax.axis_index("seq") % 2
    return jnp.where(core == 0, left, right), jnp.where(core == 0, right, left)


def pair_grad(left, right):
    mine, other = core_halves(left, right)
    return mine, exchange(other, "seq", 1)


def cut(value):
    half = value.shape[1] // 2
    return value[:, :half], value[:, half:]


def gather_seq(value):
    pieces = {0: value}
    for bit in bits_of(lax.axis_size("seq"), 2) + [1]:
        for off in list(pieces):
            pieces[off ^ bit] = exchange(pieces[off], "seq", bit)
    return [pieces[off] for off in range(len(pieces))]


def scatter_seq(mine, other):
    got = exchange(other, "seq", 1)
    size = mine.shape[0]
    total = mine[:2].astype(f32) + got[:2].astype(f32)
    for chip in range(1, size // 2):
        part = mine[2 * chip : 2 * chip + 2].astype(f32) + got[2 * chip : 2 * chip + 2].astype(f32)
        total = total + exchange(part.astype(bf16), "seq", 2 * chip).astype(f32)
    total = total.astype(bf16)
    return total[0], total[1], exchange(total[1], "seq", 1)


def sum_all(value):
    for axis, bit in [("seq", b) for b in bits_of(lax.axis_size("seq"), 1)] + [
        ("dp", b) for b in bits_of(lax.axis_size("dp"), 1)
    ]:
        value = value + exchange(value, axis, bit)
    return value


UNIT = 256


def nt(left, right):
    return lax.dot_general(left, right, (((1,), (1,)), ((), ())), preferred_element_type=f32)


def make_strip(e_ref, strip, tokens):
    heads, parts = strip.shape[0], strip.shape[1]
    for h in range(heads):
        line = e_ref[0, h : h + 1, :]
        turned = pltpu.roll(
            jnp.broadcast_to(line, (tokens, line.shape[1])), 0, 1, stride=1, stride_axis=0
        )
        for d in range(parts):
            strip[h, d] = turned[:, tokens * (d + 1) : tokens * (d + 2)]


def two_heads(ref, rows, lane, head):
    return jnp.concatenate(
        [ref[rows, lane : lane + head], ref[rows, lane + head : lane + 2 * head]], axis=0
    )


def unit_rows(refs, unit, per_unit, count, s, lane, head):
    return jnp.concatenate(
        [
            refs[unit * per_unit + p][s * count : (s + 1) * count, lane : lane + head]
            for p in range(per_unit)
        ],
        axis=0,
    )


def unit_bias(strip, me, unit, per_unit, group):
    rows = []
    for p in range(per_unit):
        place = me - (me ^ (unit * per_unit + p)) + 1
        rows.append(jnp.concatenate([strip[2 * group, place], strip[2 * group + 1, place]], axis=1))
    return jnp.concatenate(rows, axis=0)


def attend_kernel(biased, seqs, tokens, count, pieces, batch, *refs):
    info, refs = refs[0], refs[1:]
    if biased:
        e_ref, refs = refs[0], refs[1:]
    q_ref, refs = refs[0], refs[1:]
    k_refs, v_refs = refs[:pieces], refs[pieces : 2 * pieces]
    out_ref, lse_ref, peak, total, mixed, queries = refs[2 * pieces : 2 * pieces + 6]
    if biased:
        strip = refs[2 * pieces + 6]
        make_strip(e_ref, strip, tokens)
    per_unit = UNIT // count
    units = pieces // per_unit
    me = info[0]
    mine = me // per_unit
    head = q_ref.shape[1] // (2 * batch)
    for s in range(seqs):
        rows = slice(s * tokens, (s + 1) * tokens)

        @pl.when(info[1 + s] > 0)
        def _(s=s, rows=rows):
            for g in range(batch):
                queries[g] = two_heads(q_ref, rows, 2 * g * head, head) * scale
            peak[...] = jnp.full(peak.shape, -3e38, f32)
            total[...] = jnp.zeros(total.shape, f32)
            mixed[...] = jnp.zeros(mixed.shape, f32)
            for unit in range(units):
                if biased:
                    used = (unit ^ mine) <= mine
                else:
                    used = (unit ^ mine) < info[1 + s]

                @pl.when(used)
                def _(unit=unit):
                    states = []
                    for g in range(batch):
                        k = unit_rows(k_refs, unit, per_unit, count, s, g * head, head)
                        scores = nt(k, queries[g])
                        if biased:
                            scores = scores + unit_bias(strip, me, unit, per_unit, g)
                        states.append((scores, peak[g], total[g], mixed[g]))
                    done = []
                    for g, (scores, old, summed, part) in enumerate(states):
                        v = unit_rows(v_refs, unit, per_unit, count, s, g * head, head)
                        top = jnp.maximum(old, jnp.max(scores, axis=0, keepdims=True))
                        raised = jnp.exp(scores - top)
                        fade = jnp.exp(old - top)
                        done.append(
                            (
                                top,
                                summed * fade + jnp.sum(raised, axis=0, keepdims=True),
                                part * fade + mm(v.T, raised.astype(bf16)),
                            )
                        )
                    for g in range(batch):
                        peak[g], total[g], mixed[g] = done[g]

            for g in range(batch):
                lse_ref[0, batch * s + g : batch * s + g + 1, :] = peak[g] + jnp.log(total[g])
                done = (mixed[g] / total[g]).T.astype(bf16)
                out_ref[rows, 2 * g * head : 2 * (g + 1) * head] = jnp.concatenate(
                    [done[:tokens], done[tokens:]], axis=1
                )

        @pl.when(info[1 + s] <= 0)
        def _(s=s, rows=rows):
            lse_ref[0, batch * s : batch * (s + 1), :] = jnp.zeros((batch, 2 * tokens), f32)
            out_ref[rows, :] = jnp.zeros((tokens, out_ref.shape[1]), bf16)


def back_kernel(biased, seqs, tokens, count, pieces, after, batch, *refs):
    info, refs = refs[0], refs[1 + after :]
    if biased:
        e_ref, refs = refs[0], refs[1:]
    q_ref, o_ref, do_ref, lse_ref, refs = refs[0], refs[1], refs[2], refs[3], refs[4:]
    k_refs, v_refs, refs = refs[:pieces], refs[pieces : 2 * pieces], refs[2 * pieces :]
    dq_ref, keep, send, refs = refs[0], refs[1], refs[2], refs[3:]
    if biased:
        table_ref, refs = refs[0], refs[1:]
    dq, queries, grads, inner = refs[:4]
    if biased:
        strip, sums = refs[4:]
        make_strip(e_ref, strip, tokens)
        sums[...] = jnp.zeros(sums.shape, f32)
    per_unit = UNIT // count
    units = pieces // per_unit
    me = info[0]
    mine = me // per_unit
    first = me % 2 == 0
    head = q_ref.shape[1] // (2 * batch)
    for s in range(seqs):
        rows = slice(s * tokens, (s + 1) * tokens)
        keys = slice(s * count, (s + 1) * count)

        def clear(unit, keys=keys):
            for p in range(per_unit):
                piece = unit * per_unit + p
                keep[piece, keys, :] = jnp.zeros((count, batch * head), bf16)
                send[piece ^ 1, keys, :] = jnp.zeros((count, batch * head), bf16)

        @pl.when(info[1 + s] > 0)
        def _(s=s, rows=rows, keys=keys, clear=clear):
            for g in range(batch):
                lane = 2 * g * head
                queries[g] = two_heads(q_ref, rows, lane, head) * scale
                do2 = two_heads(do_ref, rows, lane, head)
                o2 = two_heads(o_ref, rows, lane, head)
                grads[g] = do2
                inner[g] = jnp.sum((o2.astype(f32) * do2.astype(f32)).T, axis=0, keepdims=True)
            dq[...] = jnp.zeros(dq.shape, f32)
            for unit in range(units):
                if biased:
                    used = (unit ^ mine) <= mine
                else:
                    used = (unit ^ mine) < info[1 + s]

                @pl.when(used)
                def _(unit=unit):
                    states = []
                    for g in range(batch):
                        k = unit_rows(k_refs, unit, per_unit, count, s, g * head, head)
                        v = unit_rows(v_refs, unit, per_unit, count, s, g * head, head)
                        scores = nt(k, queries[g])
                        if biased:
                            scores = scores + unit_bias(strip, me, unit, per_unit, g)
                        states.append((k, scores, nt(v, grads[g])))
                    done, turned = [], []
                    for g, (k, scores, down) in enumerate(states):
                        share = jnp.exp(scores - lse_ref[0, batch * s + g : batch * s + g + 1, :])
                        grad = (share * (down - inner[g])).astype(bf16)
                        dv = mm(share.astype(bf16), grads[g])
                        dk = mm(grad, queries[g])
                        turned.append(mm(k.T, grad))
                        done.append(
                            (
                                grad,
                                jnp.where(first, dk, dv).astype(bf16),
                                jnp.where(first, dv, dk).astype(bf16),
                            )
                        )
                    for g in range(batch):
                        dq[g] += turned[g]
                    kept = jnp.concatenate([d[1] for d in done], axis=1)
                    sent = jnp.concatenate([d[2] for d in done], axis=1)
                    for p in range(per_unit):
                        piece = unit * per_unit + p
                        part = slice(p * count, (p + 1) * count)
                        keep[piece, keys, :] = kept[part]
                        send[piece ^ 1, keys, :] = sent[part]
                        if biased:
                            place = me - (me ^ piece) + 1
                            for g in range(batch):
                                for h in range(2):
                                    sums[2 * g + h, place] += done[g][0][
                                        part, h * tokens : (h + 1) * tokens
                                    ].astype(f32)

                @pl.when(jnp.logical_not(used))
                def _(unit=unit):
                    clear(unit)

            for g in range(batch):
                done = (dq[g] * scale).T.astype(bf16)
                dq_ref[rows, 2 * g * head : 2 * (g + 1) * head] = jnp.concatenate(
                    [done[:tokens], done[tokens:]], axis=1
                )

        @pl.when(info[1 + s] <= 0)
        def _(rows=rows, clear=clear):
            for unit in range(units):
                clear(unit)
            dq_ref[rows, :] = jnp.zeros((tokens, dq_ref.shape[1]), bf16)

    if biased:
        parts = sums.shape[1]
        span = tokens * (parts + 1)
        for h in range(2 * batch):
            line = jnp.concatenate(
                [jnp.zeros((tokens, tokens), f32)] + [sums[h, d] for d in range(parts)], axis=1
            )
            height = tokens
            while height > 8:
                height = height // 2
                line = line[:height] + pltpu.roll(line[height:], span - height, 1)
            while height > 1:
                height = height // 2
                upper = pltpu.roll(line, span - height, 1)
                line = line[:height] + upper[height : 2 * height]
            table_ref[0, h : h + 1, :] = line


def block_of(array, lanes, offset=0):
    return pl.BlockSpec((array.shape[0], lanes), lambda i, info: (0, offset + i))


BATCH = 4


def attend(query, pieces, info, seqs, line):
    tokens = query.shape[0] // seqs
    count = pieces[0].shape[0] // seqs
    n = len(pieces)
    steps = GROUPS // BATCH
    wide, narrow = query.shape[1] // steps, pieces[0].shape[1] // 2 // steps
    head = narrow // BATCH
    biased = line is not None
    scratch = [pltpu.VMEM((BATCH, 1, 2 * tokens), f32)] * 2 + [
        pltpu.VMEM((BATCH, head, 2 * tokens), f32),
        pltpu.VMEM((BATCH, 2 * tokens, head), bf16),
    ]
    extra = []
    if biased:
        scratch.append(pltpu.VMEM((2 * BATCH, n + 1, tokens, tokens), f32))
        extra = [pl.BlockSpec((1, 2 * BATCH, line.shape[2]), lambda i, info: (i, 0, 0))]
    pairs = n * count * seqs * tokens * GROUPS * 2
    return pl.pallas_call(
        functools.partial(attend_kernel, biased, seqs, tokens, count, n, BATCH),
        grid_spec=pltpu.PrefetchScalarGridSpec(
            num_scalar_prefetch=1,
            grid=(steps,),
            in_specs=extra
            + [block_of(query, wide)]
            + [block_of(p, narrow) for p in pieces]
            + [block_of(p, narrow, steps) for p in pieces],
            out_specs=[
                block_of(query, wide),
                pl.BlockSpec((1, BATCH * seqs, 2 * tokens), lambda i, info: (i, 0, 0)),
            ],
            scratch_shapes=scratch,
        ),
        out_shape=[
            jax.ShapeDtypeStruct(query.shape, bf16),
            jax.ShapeDtypeStruct((steps, BATCH * seqs, 2 * tokens), f32),
        ],
        compiler_params=pltpu.CompilerParams(vmem_limit_bytes=40 * 1024 * 1024),
        cost_estimate=pl.CostEstimate(
            flops=256 * pairs, bytes_accessed=4 * query.size + 2 * n * pieces[0].size, transcendentals=pairs
        ),
    )(info, *([line] if biased else []), query, *pieces, *pieces)


def attend_back(query, mixed, upstream, logsum, pieces, info, seqs, line, after=()):
    tokens = query.shape[0] // seqs
    count = pieces[0].shape[0] // seqs
    n = len(pieces)
    steps = GROUPS // BATCH
    wide, narrow = query.shape[1] // steps, pieces[0].shape[1] // 2 // steps
    head = narrow // BATCH
    biased = line is not None
    scratch = [
        pltpu.VMEM((BATCH, head, 2 * tokens), f32),
        pltpu.VMEM((BATCH, 2 * tokens, head), bf16),
        pltpu.VMEM((BATCH, 2 * tokens, head), bf16),
        pltpu.VMEM((BATCH, 1, 2 * tokens), f32),
    ]
    extra, extra_out, extra_shape = [], [], []
    if biased:
        scratch += [pltpu.VMEM((2 * BATCH, n + 1, tokens, tokens), f32)] * 2
        extra = [pl.BlockSpec((1, 2 * BATCH, line.shape[2]), lambda i, info: (i, 0, 0))]
        extra_out = [pl.BlockSpec((1, 2 * BATCH, tokens * (n + 2)), lambda i, info: (i, 0, 0))]
        extra_shape = [jax.ShapeDtypeStruct((steps, 2 * BATCH, tokens * (n + 2)), f32)]
    part = pl.BlockSpec((n, seqs * count, narrow), lambda i, info: (0, 0, i))
    part_shape = jax.ShapeDtypeStruct((n, seqs * count, narrow * steps), bf16)
    pairs = n * count * seqs * tokens * GROUPS * 2
    return pl.pallas_call(
        functools.partial(back_kernel, biased, seqs, tokens, count, n, len(after), BATCH),
        grid_spec=pltpu.PrefetchScalarGridSpec(
            num_scalar_prefetch=1,
            grid=(steps,),
            in_specs=[pl.BlockSpec(memory_space=pl.ANY)] * len(after)
            + extra
            + [block_of(query, wide)] * 3
            + [pl.BlockSpec((1, BATCH * seqs, 2 * tokens), lambda i, info: (i, 0, 0))]
            + [block_of(p, narrow) for p in pieces]
            + [block_of(p, narrow, steps) for p in pieces],
            out_specs=[block_of(query, wide), part, part] + extra_out,
            scratch_shapes=scratch,
        ),
        out_shape=[jax.ShapeDtypeStruct(query.shape, bf16), part_shape, part_shape] + extra_shape,
        compiler_params=pltpu.CompilerParams(vmem_limit_bytes=44 * 1024 * 1024),
        cost_estimate=pl.CostEstimate(
            flops=640 * pairs, bytes_accessed=8 * query.size + 6 * n * pieces[0].size, transcendentals=pairs
        ),
    )(info, *after, *([line] if biased else []), query, mixed, upstream, logsum, *pieces, *pieces)


def feed_kernel(core_ref, second, live, gain, normed, grad_low, gate_w, up_w, down_w, hidden, own, pair, outputs, grad, gain_grad, result, feed_in):
    step = pl.program_id(0)

    @pl.when(step == 0)
    def _():
        result[...] = jnp.zeros(result.shape, f32)
        feed_in[...] = jnp.zeros(feed_in.shape, f32)

    gate = mm(normed[...], gate_w[...])
    upper = mm(normed[...], up_w[...])
    incoming = nt(grad_low[...], down_w[...])
    square = gate * gate
    slope = 0.7978845608028654 * 0.044715
    bend = jnp.tanh(gate * (0.7978845608028654 + slope * square))
    rise = 0.5 * (1.0 + bend)
    curve = gate * rise
    steep = rise + 0.5 * gate * (1.0 - bend * bend) * (0.7978845608028654 + 3.0 * slope * square)
    acted = (curve * upper).astype(bf16)
    gate_grad = (incoming * upper * steep).astype(bf16)
    upper_grad = (incoming * curve).astype(bf16)
    hidden[...] = acted
    first = core_ref[0] == 0
    own[...] = jnp.where(first, gate_grad, upper_grad)
    pair[...] = jnp.where(first, upper_grad, gate_grad)
    result[...] += mm(acted, down_w[...])
    feed_in[...] += nt(gate_grad, gate_w[...]) + nt(upper_grad, up_w[...])

    @pl.when(step == pl.num_programs(0) - 1)
    def _():
        value = second[...]
        outputs[...] = ((value + result[...]) * live[...]).astype(bf16)
        rate = norm_rate(value)
        scaled = feed_in[...] * gain[...]
        inner = jnp.mean(scaled * value, axis=-1, keepdims=True)
        grad[...] = grad_low[...].astype(f32) + rate * (scaled - value * (rate * rate * inner))
        gain_grad[...] = jnp.sum(feed_in[...] * value * rate, axis=0, keepdims=True)


def feed_forward(core, second, live, gain, normed, grad_low, gate_weight, up_weight, down_weight):
    tokens, width = second.shape
    units = gate_weight.shape[1]
    whole = pl.BlockSpec((tokens, width), lambda i: (0, 0))
    line = pl.BlockSpec((1, width), lambda i: (0, 0))
    tall = pl.BlockSpec((width, TILE), lambda i: (0, i))
    part = pl.BlockSpec((tokens, TILE), lambda i: (0, i))
    part_shape = jax.ShapeDtypeStruct((tokens, units), bf16)
    return pl.pallas_call(
        feed_kernel,
        grid=(units // TILE,),
        in_specs=[
            pl.BlockSpec(memory_space=pltpu.SMEM),
            whole,
            pl.BlockSpec((tokens, 1), lambda i: (0, 0)),
            line,
            whole,
            whole,
            tall,
            tall,
            pl.BlockSpec((TILE, width), lambda i: (i, 0)),
        ],
        out_specs=[part, part, part, whole, whole, line],
        out_shape=[part_shape] * 3
        + [
            jax.ShapeDtypeStruct((tokens, width), bf16),
            jax.ShapeDtypeStruct((tokens, width), f32),
            jax.ShapeDtypeStruct((1, width), f32),
        ],
        scratch_shapes=[pltpu.VMEM((tokens, width), f32)] * 2,
        compiler_params=pltpu.CompilerParams(vmem_limit_bytes=32 * 1024 * 1024),
        cost_estimate=pl.CostEstimate(
            flops=12 * tokens * width * units,
            bytes_accessed=6 * width * units + 6 * tokens * units + 14 * tokens * width,
            transcendentals=tokens * units,
        ),
    )(core, second, live, gain.reshape(1, -1), normed, grad_low, gate_weight, up_weight, down_weight)


def per_device(
    inputs,
    memory,
    target_length,
    memory_length,
    distance_bucket,
    bias_table,
    self_gain,
    self_query,
    self_key,
    self_value,
    self_out,
    cross_gain,
    cross_query,
    cross_key,
    cross_value,
    cross_out,
    feed_gain,
    gate_weight,
    up_weight,
    down_weight,
    upstream,
):
    tokens, seqs, width = inputs.shape
    mem_tokens = memory.shape[0]
    size = lax.axis_size("seq")
    length = tokens * size
    buckets = bias_table.shape[0]
    me = lax.axis_index("seq")

    def flat(array):
        return jnp.transpose(array, (1, 0, 2)).reshape(-1, array.shape[2])

    def unflat(array):
        return jnp.transpose(array.reshape(seqs, -1, array.shape[1]), (1, 0, 2))

    positions = me * tokens + jnp.arange(tokens, dtype=jnp.int32)
    live = (positions[None, :] < target_length[:, None]).reshape(-1, 1)
    held = me * mem_tokens + jnp.arange(mem_tokens, dtype=jnp.int32)
    held = (held[None, :] < memory_length[:, None]).reshape(-1, 1)
    me_line = me.astype(jnp.int32).reshape(1)
    self_info = jnp.concatenate([me_line, (me * tokens < target_length).astype(jnp.int32)])
    cross_info = jnp.concatenate([me_line, (memory_length + UNIT - 1) // UNIT])

    x = flat(inputs)
    xf = x.astype(f32)
    mem = jnp.where(held, flat(memory), 0)
    grad_low = jnp.where(live, flat(upstream), 0)
    rate_self = norm_rate(xf)
    normed_self = (xf * rate_self * self_gain).astype(bf16)
    keys = mm(normed_self, self_key).astype(bf16)
    values = mm(normed_self, self_value).astype(bf16)
    gathered = gather_seq(jnp.concatenate([keys, values], axis=1))
    memory_kv = jnp.concatenate(
        [mm(mem, cross_key).astype(bf16), mm(mem, cross_value).astype(bf16)], axis=1
    )
    recalled = gather_seq(memory_kv)
    query = mm(normed_self, self_query).astype(bf16)

    bucket_match = distance_bucket[:, None] == jnp.arange(buckets, dtype=jnp.int32)[None, :]
    bucket_onehot = bucket_match.astype(f32)
    line = jnp.dot(bias_table.T, bucket_onehot.T, precision=highest, preferred_element_type=f32)
    line = jnp.concatenate([jnp.full((line.shape[0], 2 * tokens), negative, f32), line], axis=1)
    line = line.reshape(GROUPS // BATCH, -1, length + 2 * tokens)

    self_mixed, self_logsum = attend(query, gathered, self_info, seqs, line)
    first = xf + mm(self_mixed, self_out)
    rate_cross = norm_rate(first)
    normed_cross = (first * rate_cross * cross_gain).astype(bf16)
    recall_query = mm(normed_cross, cross_query).astype(bf16)
    cross_mixed, cross_logsum = attend(recall_query, recalled, cross_info, seqs, None)
    second = first + mm(cross_mixed, cross_out)
    rate_feed = norm_rate(second)
    normed_feed = (second * rate_feed * feed_gain).astype(bf16)
    core = (me % 2).astype(jnp.int32).reshape(1)
    hidden, gu_own, gu_other, outputs, second_grad, feed_gain_grad = feed_forward(
        core, second, live.astype(f32), feed_gain, normed_feed, grad_low, gate_weight, up_weight, down_weight
    )
    feed_gain_grad = feed_gain_grad.reshape(-1)
    low_own, low_pair = pair_grad(*cut(grad_low))
    mem_pair = exchange(mem, "seq", 1)
    shared = exchange(
        jnp.concatenate([normed_self, self_mixed, normed_cross, cross_mixed, normed_feed], axis=1), "seq", 1
    )
    hidden_pair = exchange(hidden, "seq", 1)
    gu_pair = exchange(gu_other, "seq", 1)
    hidden_cols = hidden.shape[1]
    tiles = hidden_cols // TILE
    cutting = tiles // 2
    second_low = second_grad.astype(bf16)
    cross_mixed_grad = mm_t(second_low, cross_out).astype(bf16)
    recall_query_grad, kept, sent = attend_back(
        recall_query, cross_mixed, cross_mixed_grad, cross_logsum, recalled, cross_info, seqs, None
    )
    gu_task = (((1, 0), (2, 4 * width), (5, 0), (6, 0)), width)
    feed_chain = Chain(
        group_grads(
            [hidden, normed_feed, shared, low_own, low_pair, gu_own, gu_pair, hidden_pair],
            [
                gu_task + ([(0, j * TILE) for j in range(cutting)],),
                gu_task + ([(1, j * TILE) for j in range(cutting, tiles)],),
                (((0, 0), (7, 0), (3, 0), (4, 0)), hidden_cols, [(0, 0), (1, TILE)]),
            ],
            [recall_query_grad],
        )
    )
    early = list(feed_chain.send)
    feed_first = feed_chain.step()
    memory_half, memory_half_pair, memory_other = scatter_seq(kept, sent)
    cross_in = mm_t(recall_query_grad, cross_query)
    first_part, cross_gain_grad = norm_back(first, rate_cross, cross_gain, cross_in)
    first_grad = second_grad + first_part
    first_low = first_grad.astype(bf16)
    self_mixed_grad = mm_t(first_low, self_out).astype(bf16)
    halves = [core_halves(*cut(v)) for v in (second_low, recall_query_grad, first_low)]
    grads_own = jnp.concatenate([h[0] for h in halves], axis=1)
    grads_pair = exchange(jnp.concatenate([h[1] for h in halves], axis=1), "seq", 1)
    memory_key_low, memory_value_low = core_halves(memory_half, memory_other)
    memory_grad = mm_t(memory_key_low, cross_key) + mm_t(memory_value_low, cross_value)

    query_grad, kept, sent, line_grad = attend_back(
        query, self_mixed, self_mixed_grad, self_logsum, gathered, self_info, seqs, line, early
    )
    line_grad = line_grad.reshape(-1, line_grad.shape[2])[:, 2 * tokens :]
    table_grad = jnp.dot(line_grad, bucket_onehot, precision=highest, preferred_element_type=f32).T
    key_half, key_half_pair, key_other = scatter_seq(kept, sent)
    two = [(0, 0), (1, TILE)]
    out_chain = Chain(
        group_grads(
            [cross_mixed, normed_cross, self_mixed, shared, mem, mem_pair, grads_own, grads_pair, memory_half, memory_half_pair],
            [
                (((0, 0), (3, 3 * width), (6, 0), (7, 0)), width, two),
                (((1, 0), (3, 2 * width), (6, width // 2), (7, width // 2)), width, two),
                (((2, 0), (3, width), (6, width), (7, width)), width, two),
                (((4, 0), (5, 0), (8, 0), (9, 0)), width, two),
            ],
            [query_grad] + feed_first,
        )
    )
    query_own, query_pair = pair_grad(*cut(query_grad))
    in_chain = Chain(
        group_grads(
            [normed_self, shared, query_own, query_pair, key_half, key_half_pair],
            [
                (((0, 0), (1, 0), (2, 0), (3, 0)), width, two),
                (((0, 0), (1, 0), (4, 0), (5, 0)), width, two),
            ],
            [out_chain.send[0]],
        )
    )
    key_low, value_low = core_halves(key_half, key_other)
    self_in = mm_t(query_grad, self_query) + mm_t(key_low, self_key) + mm_t(value_low, self_value)
    input_part, self_gain_grad = norm_back(xf, rate_self, self_gain, self_in)
    input_grad = first_grad + input_part
    small = jnp.concatenate(
        [self_gain_grad, cross_gain_grad, feed_gain_grad, table_grad.reshape(-1)]
    ).reshape(-1, 128)
    small = sum_all(small).reshape(-1)

    blocks = 2 ** len(grad_order(False))
    narrow, broad = width // blocks, hidden_cols // blocks
    piece = feed_chain.finish()
    middle = cutting * narrow
    feed_tiles = jnp.concatenate([piece[:middle], piece[middle + broad : -broad]], axis=0)
    down_tiles = jnp.concatenate([piece[middle : middle + broad], piece[-broad:]], axis=0)
    (gate_out, up_out), down_out = swap_rows(
        [
            feed_tiles.reshape(tiles, narrow, TILE),
            down_tiles.reshape(2, broad, TILE),
        ]
    )

    def by_weight(piece):
        stacks = piece.reshape(2, -1, narrow, TILE)
        return swap_rows([stacks[:, i] for i in range(stacks.shape[1])])

    cross_out_out, cross_query_out, self_out_out, cross_kv_out = by_weight(out_chain.finish())
    self_query_out, self_kv_out = by_weight(in_chain.finish())

    def joined(pair):
        return jnp.concatenate(pair, axis=1)

    return (
        unflat(outputs),
        unflat(input_grad),
        unflat(memory_grad),
        small[:width],
        joined(self_query_out),
        self_kv_out[0],
        self_kv_out[1],
        joined(self_out_out),
        small[3 * width :].reshape(buckets, -1),
        small[width : 2 * width],
        joined(cross_query_out),
        cross_kv_out[0],
        cross_kv_out[1],
        joined(cross_out_out),
        small[2 * width : 3 * width],
        gate_out,
        up_out,
        joined(down_out),
    )


def solution(mesh):
    placed = P("seq", "dp", None)
    rows = P(("dp", "seq"), None)
    return jax.shard_map(
        per_device,
        mesh=mesh,
        in_specs=(placed, placed, P("dp"), P("dp")) + (P(),) * 16 + (placed,),
        out_specs=(
            placed,
            placed,
            placed,
            P(),
            rows,
            rows,
            rows,
            rows,
            P(),
            P(),
            rows,
            rows,
            rows,
            rows,
            P(),
            rows,
            rows,
            rows,
        ),
        check_vma=False,
    )
```

```python
import functools

import jax
import jax.numpy as jnp
from jax import lax
from jax.experimental import pallas as pl
from jax.experimental.pallas import tpu as pltpu
from jax.sharding import PartitionSpec as P

GROUPS = 8


epsilon = 1e-06
scale = 0.125
negative = -1e30
highest = lax.Precision.HIGHEST
bf16 = jnp.bfloat16
f32 = jnp.float32


def norm_rate(value):
    return lax.rsqrt(jnp.mean(value * value, axis=-1, keepdims=True) + epsilon)


def norm_back(value, rate, gain, incoming):
    scaled = incoming * gain
    inner = jnp.mean(scaled * value, axis=-1, keepdims=True)
    grad = rate * (scaled - value * (rate * rate * inner))
    return grad, jnp.sum(incoming * value * rate, axis=0, keepdims=True)


def mm(left, right):
    return jnp.dot(left, right, preferred_element_type=f32)


def mm_t(grad, weight):
    return lax.dot_general(grad, weight, (((1,), (1,)), ((), ())), preferred_element_type=f32)


def exchange(value, axis, bit):
    size = lax.axis_size(axis)
    return lax.ppermute(value, axis, [(i, i ^ bit) for i in range(size)])


def bits_of(size, lowest):
    bits = []
    bit = lowest
    while bit < size:
        bits.append(bit)
        bit = bit * 2
    return bits


TILE = 256
LIGHT = pl.CostEstimate(flops=1, bytes_accessed=1, transcendentals=0)


def grad_order(flip):
    seq_bits = bits_of(lax.axis_size("seq"), 2)
    if flip:
        seq_bits = seq_bits[::-1]
    return [("seq", b) for b in seq_bits] + [("dp", b) for b in bits_of(lax.axis_size("dp"), 1)]


def grads_kernel(chips, orders, tasks, sources, count, me_ref, *refs):
    ins, refs = refs[:sources], refs[count:]
    outs, (turned, total) = refs[:4], refs[4:]
    blocks = 2 ** len(orders[0])
    filled = [0, 0]
    for (xo, xp, do, dp), tokens, rows, rchip, tiles in tasks:
        for half, (place, lane) in enumerate((xo, xp)):
            turned[:rows, half * tokens : (half + 1) * tokens] = ins[place][:, lane : lane + rows].T
        for stack, lane in tiles:
            value = mm(turned[:rows, :tokens], ins[do[0]][:, do[1] + lane : do[1] + lane + TILE])
            value = value + mm(
                turned[:rows, tokens : 2 * tokens], ins[dp[0]][:, dp[1] + lane : dp[1] + lane + TILE]
            )
            for block in range(blocks):
                total[block, :rchip] = value[block * rchip : (block + 1) * rchip]
            order = orders[stack]
            for slot in range(blocks):
                seq_part, dp_part = 0, 0
                for place, (axis, bit) in enumerate(order):
                    if (slot >> (len(order) - 1 - place)) & 1:
                        if axis == "seq":
                            seq_part = seq_part | (bit // 2)
                        else:
                            dp_part = dp_part | bit
                block = (me_ref[0] ^ dp_part) * chips + (me_ref[1] ^ seq_part)
                outs[2 * stack + slot // (blocks // 2)][
                    slot % (blocks // 2), filled[stack] : filled[stack] + rchip
                ] = total[block, :rchip].astype(bf16)
            filled[stack] += rchip


def group_grads(arrays, tasks, after=()):
    chips = lax.axis_size("seq") // 2
    orders = [grad_order(False), grad_order(True)]
    blocks = 2 ** len(orders[0])
    full = []
    depth = [0, 0]
    flops = 0
    for names, rows, tiles in tasks:
        tokens = arrays[names[0][0]].shape[0]
        full.append((names, tokens, rows, rows // blocks, tiles))
        flops += 4 * tokens * rows * TILE * len(tiles)
        for stack, lane in tiles:
            depth[stack] += rows // blocks
    me = jnp.stack([lax.axis_index("dp"), lax.axis_index("seq") // 2]).astype(jnp.int32)
    vmem = pl.BlockSpec(memory_space=pltpu.VMEM)
    most = max(t[2] for t in full)
    shapes = [jax.ShapeDtypeStruct((blocks // 2, depth[i // 2], TILE), bf16) for i in range(4)]
    total = arrays[0].dtype.itemsize * sum(a.size for a in arrays)
    return pl.pallas_call(
        functools.partial(grads_kernel, chips, orders, full, len(arrays), len(arrays) + len(after)),
        in_specs=[pl.BlockSpec(memory_space=pltpu.SMEM)]
        + [vmem] * len(arrays)
        + [pl.BlockSpec(memory_space=pl.ANY)] * len(after),
        out_specs=[vmem] * 4,
        scratch_shapes=[
            pltpu.VMEM((most, max(2 * t[1] for t in full)), bf16),
            pltpu.VMEM((blocks, most // blocks, TILE), f32),
        ],
        out_shape=shapes,
        compiler_params=pltpu.CompilerParams(vmem_limit_bytes=44 * 1024 * 1024),
        cost_estimate=LIGHT,
    )(me, *arrays, *after)


class Chain:
    def __init__(self, keep, send, orders, level=0):
        self.keep, self.send, self.orders, self.level, self.got = keep, send, orders, level, None

    @staticmethod
    def of(outs):
        return Chain([outs[0], outs[2]], [outs[1], outs[3]], [grad_order(False), grad_order(True)])

    @staticmethod
    def merged(chains):
        level = chains[0].level
        if chains[0].orders[0][level][0] == "dp":
            keeps = [[k for c in chains for k in c.keep]]
            sends = [[v for c in chains for v in c.send]]
        else:
            keeps = [list(k) for k in zip(*[c.keep for c in chains])]
            sends = [list(v) for v in zip(*[c.send for c in chains])]
        joined = [[jnp.concatenate(v, axis=1) for v in group] for group in (keeps, sends)]
        return Chain(joined[0], joined[1], chains[0].orders[: len(keeps)], level)

    def start(self, tokens=()):
        if tokens:
            self.send = tie(self.send, tokens)
        self.got = [exchange(v, *self.orders[i][self.level]) for i, v in enumerate(self.send)]
        self.level += 1
        return self.got

    def add(self):
        got, self.got = self.got, None
        half = got[0].shape[0] // 2
        if half:
            self.send = [k[half:] + g[half:] for k, g in zip(self.keep, got)]
            self.keep = [k[:half] + g[:half] for k, g in zip(self.keep, got)]
        else:
            self.keep = [k.astype(f32) + g.astype(f32) for k, g in zip(self.keep, got)]

    def to_dp(self):
        while self.orders[0][self.level][0] == "seq":
            self.start()
            self.add()

    def finish(self):
        if self.got is not None:
            self.add()
        while self.level < len(self.orders[0]):
            self.start()
            self.add()
        return self.keep[0][0]


def swap_rows(parts):
    lows, highs = [], []
    for part in parts:
        half = part.shape[1] // 2
        lows.append(part[:, :half].reshape(-1, TILE))
        highs.append(part[:, half:].reshape(-1, TILE))
    low = jnp.concatenate(lows, axis=0)
    high = jnp.concatenate(highs, axis=0)
    mine, other = core_halves(low, high)
    got = exchange(other.astype(bf16), "seq", 1).astype(f32)
    first, second = core_halves(mine, got)
    done = []
    start = 0
    for part in parts:
        tiles, half = part.shape[0], part.shape[1] // 2
        pair = []
        for whole in (first, second):
            piece = whole[start : start + tiles * half].reshape(tiles, half, TILE)
            pair.append(jnp.transpose(piece, (1, 0, 2)).reshape(half, tiles * TILE))
        done.append(tuple(pair))
        start += tiles * half
    return done


def core_halves(left, right):
    core = lax.axis_index("seq") % 2
    return jnp.where(core == 0, left, right), jnp.where(core == 0, right, left)


def pair_grad(left, right):
    mine, other = core_halves(left, right)
    return mine, exchange(other, "seq", 1)


def cut(value):
    half = value.shape[1] // 2
    return value[:, :half], value[:, half:]


def tie(values, tokens):
    done = lax.optimization_barrier((tuple(values), tuple(tokens)))
    return list(done[0])


def gather_start(value):
    chips = lax.axis_size("seq") // 2
    return [value] + [exchange(value, "seq", 2 * chip) for chip in range(1, chips)]


def gather_finish(mine):
    own = exchange(mine[0], "seq", 1)
    rest = exchange(jnp.concatenate(mine[1:], axis=1), "seq", 1)
    pieces = []
    for chip, value in enumerate(mine):
        pieces.append((value, 0))
        pieces.append((own, 0) if chip == 0 else (rest, chip - 1))
    return pieces


def scatter_start(mine, other):
    got = exchange(other, "seq", 1)
    parts = []
    for chip in range(mine.shape[0] // 2):
        pair = slice(2 * chip, 2 * chip + 2)
        part = mine[pair].astype(f32) + got[pair].astype(f32)
        parts.append(part if chip == 0 else part.astype(bf16))
    return parts


def scatter_send(parts):
    return [exchange(part, "seq", 2 * (chip + 1)) for chip, part in enumerate(parts[1:])]


def scatter_finish(part, arrived):
    total = part
    for value in arrived:
        total = total + value.astype(f32)
    total = total.astype(bf16)
    return total[0], total[1], exchange(total[1], "seq", 1)


def sum_over(value, steps):
    for axis, bit in steps:
        value = value + exchange(value, axis, bit)
    return value


UNIT = 256


def nt(left, right):
    return lax.dot_general(left, right, (((1,), (1,)), ((), ())), preferred_element_type=f32)


def make_strip(e_ref, strip, tokens):
    heads, parts = strip.shape[0], strip.shape[1]
    for h in range(heads):
        line = e_ref[0, h : h + 1, :]
        turned = pltpu.roll(
            jnp.broadcast_to(line, (tokens, line.shape[1])), 0, 1, stride=1, stride_axis=0
        )
        for d in range(parts):
            strip[h, d] = turned[:, tokens * (d + 1) : tokens * (d + 2)]


def two_heads(ref, rows, lane, head):
    return jnp.concatenate(
        [ref[rows, lane : lane + head], ref[rows, lane + head : lane + 2 * head]], axis=0
    )


def unit_rows(refs, unit, per_unit, count, s, lane, head):
    return jnp.concatenate(
        [
            refs[unit * per_unit + p][s * count : (s + 1) * count, lane : lane + head]
            for p in range(per_unit)
        ],
        axis=0,
    )


def unit_bias(strip, me, unit, per_unit, group):
    rows = []
    for p in range(per_unit):
        place = me - (me ^ (unit * per_unit + p)) + 1
        rows.append(jnp.concatenate([strip[2 * group, place], strip[2 * group + 1, place]], axis=1))
    return jnp.concatenate(rows, axis=0)


def attend_kernel(biased, seqs, tokens, count, pieces, batch, *refs):
    info, refs = refs[0], refs[1:]
    if biased:
        e_ref, refs = refs[0], refs[1:]
    q_ref, refs = refs[0], refs[1:]
    k_refs, v_refs = refs[:pieces], refs[pieces : 2 * pieces]
    out_ref, lse_ref, peak, total, mixed, queries = refs[2 * pieces : 2 * pieces + 6]
    if biased:
        strip = refs[2 * pieces + 6]
        make_strip(e_ref, strip, tokens)
    per_unit = UNIT // count
    units = pieces // per_unit
    me = info[0]
    mine = me // per_unit
    head = q_ref.shape[1] // (2 * batch)
    for s in range(seqs):
        rows = slice(s * tokens, (s + 1) * tokens)

        @pl.when(info[1 + s] > 0)
        def _(s=s, rows=rows):
            for g in range(batch):
                queries[g] = two_heads(q_ref, rows, 2 * g * head, head) * scale
            peak[...] = jnp.full(peak.shape, -3e38, f32)
            total[...] = jnp.zeros(total.shape, f32)
            mixed[...] = jnp.zeros(mixed.shape, f32)
            for unit in range(units):
                if biased:
                    used = (unit ^ mine) <= mine
                else:
                    used = (unit ^ mine) < info[1 + s]

                @pl.when(used)
                def _(unit=unit):
                    states = []
                    for g in range(batch):
                        k = unit_rows(k_refs, unit, per_unit, count, s, g * head, head)
                        scores = nt(k, queries[g])
                        if biased:
                            scores = scores + unit_bias(strip, me, unit, per_unit, g)
                        states.append((scores, peak[g], total[g], mixed[g]))
                    done = []
                    for g, (scores, old, summed, part) in enumerate(states):
                        v = unit_rows(v_refs, unit, per_unit, count, s, g * head, head)
                        top = jnp.maximum(old, jnp.max(scores, axis=0, keepdims=True))
                        raised = jnp.exp(scores - top)
                        fade = jnp.exp(old - top)
                        done.append(
                            (
                                top,
                                summed * fade + jnp.sum(raised, axis=0, keepdims=True),
                                part * fade + mm(v.T, raised.astype(bf16)),
                            )
                        )
                    for g in range(batch):
                        peak[g], total[g], mixed[g] = done[g]

            for g in range(batch):
                lse_ref[0, batch * s + g : batch * s + g + 1, :] = peak[g] + jnp.log(total[g])
                done = (mixed[g] / total[g]).T.astype(bf16)
                out_ref[rows, 2 * g * head : 2 * (g + 1) * head] = jnp.concatenate(
                    [done[:tokens], done[tokens:]], axis=1
                )

        @pl.when(info[1 + s] <= 0)
        def _(s=s, rows=rows):
            lse_ref[0, batch * s : batch * (s + 1), :] = jnp.zeros((batch, 2 * tokens), f32)
            out_ref[rows, :] = jnp.zeros((tokens, out_ref.shape[1]), bf16)


def back_kernel(biased, seqs, tokens, count, pieces, after, batch, *refs):
    info, refs = refs[0], refs[1 + after :]
    if biased:
        e_ref, refs = refs[0], refs[1:]
    q_ref, o_ref, do_ref, lse_ref, refs = refs[0], refs[1], refs[2], refs[3], refs[4:]
    k_refs, v_refs, refs = refs[:pieces], refs[pieces : 2 * pieces], refs[2 * pieces :]
    dq_ref, keep, send, refs = refs[0], refs[1], refs[2], refs[3:]
    if biased:
        table_ref, refs = refs[0], refs[1:]
    dq, queries, grads, inner = refs[:4]
    if biased:
        strip, sums = refs[4:]
        make_strip(e_ref, strip, tokens)
        sums[...] = jnp.zeros(sums.shape, f32)
    per_unit = UNIT // count
    units = pieces // per_unit
    me = info[0]
    mine = me // per_unit
    first = me % 2 == 0
    head = q_ref.shape[1] // (2 * batch)
    for s in range(seqs):
        rows = slice(s * tokens, (s + 1) * tokens)
        keys = slice(s * count, (s + 1) * count)

        def clear(unit, keys=keys):
            for p in range(per_unit):
                piece = unit * per_unit + p
                keep[piece, keys, :] = jnp.zeros((count, batch * head), bf16)
                send[piece ^ 1, keys, :] = jnp.zeros((count, batch * head), bf16)

        @pl.when(info[1 + s] > 0)
        def _(s=s, rows=rows, keys=keys, clear=clear):
            for g in range(batch):
                lane = 2 * g * head
                queries[g] = two_heads(q_ref, rows, lane, head) * scale
                do2 = two_heads(do_ref, rows, lane, head)
                o2 = two_heads(o_ref, rows, lane, head)
                grads[g] = do2
                inner[g] = jnp.sum((o2.astype(f32) * do2.astype(f32)).T, axis=0, keepdims=True)
            dq[...] = jnp.zeros(dq.shape, f32)
            for unit in range(units):
                if biased:
                    used = (unit ^ mine) <= mine
                else:
                    used = (unit ^ mine) < info[1 + s]

                @pl.when(used)
                def _(unit=unit):
                    states = []
                    for g in range(batch):
                        k = unit_rows(k_refs, unit, per_unit, count, s, g * head, head)
                        v = unit_rows(v_refs, unit, per_unit, count, s, g * head, head)
                        scores = nt(k, queries[g])
                        if biased:
                            scores = scores + unit_bias(strip, me, unit, per_unit, g)
                        states.append((k, scores, nt(v, grads[g])))
                    done, turned = [], []
                    for g, (k, scores, down) in enumerate(states):
                        share = jnp.exp(scores - lse_ref[0, batch * s + g : batch * s + g + 1, :])
                        grad = (share * (down - inner[g])).astype(bf16)
                        dv = mm(share.astype(bf16), grads[g])
                        dk = mm(grad, queries[g])
                        turned.append(mm(k.T, grad))
                        done.append(
                            (
                                grad,
                                jnp.where(first, dk, dv).astype(bf16),
                                jnp.where(first, dv, dk).astype(bf16),
                            )
                        )
                    for g in range(batch):
                        dq[g] += turned[g]
                    kept = jnp.concatenate([d[1] for d in done], axis=1)
                    sent = jnp.concatenate([d[2] for d in done], axis=1)
                    for p in range(per_unit):
                        piece = unit * per_unit + p
                        part = slice(p * count, (p + 1) * count)
                        keep[piece, keys, :] = kept[part]
                        send[piece ^ 1, keys, :] = sent[part]
                        if biased:
                            place = me - (me ^ piece) + 1
                            for g in range(batch):
                                for h in range(2):
                                    sums[2 * g + h, place] += done[g][0][
                                        part, h * tokens : (h + 1) * tokens
                                    ].astype(f32)

                @pl.when(jnp.logical_not(used))
                def _(unit=unit):
                    clear(unit)

            for g in range(batch):
                done = (dq[g] * scale).T.astype(bf16)
                dq_ref[rows, 2 * g * head : 2 * (g + 1) * head] = jnp.concatenate(
                    [done[:tokens], done[tokens:]], axis=1
                )

        @pl.when(info[1 + s] <= 0)
        def _(rows=rows, clear=clear):
            for unit in range(units):
                clear(unit)
            dq_ref[rows, :] = jnp.zeros((tokens, dq_ref.shape[1]), bf16)

    if biased:
        parts = sums.shape[1]
        span = tokens * (parts + 1)
        for h in range(2 * batch):
            line = jnp.concatenate(
                [jnp.zeros((tokens, tokens), f32)] + [sums[h, d] for d in range(parts)], axis=1
            )
            height = tokens
            while height > 8:
                height = height // 2
                line = line[:height] + pltpu.roll(line[height:], span - height, 1)
            while height > 1:
                height = height // 2
                upper = pltpu.roll(line, span - height, 1)
                line = line[:height] + upper[height : 2 * height]
            table_ref[0, h : h + 1, :] = line


def block_of(array, lanes, offset=0):
    return pl.BlockSpec((array.shape[0], lanes), lambda i, info: (0, offset + i))


BATCH = 4


def attend(query, pieces, info, seqs, line):
    tokens = query.shape[0] // seqs
    arrays = [p[0] for p in pieces]
    count = arrays[0].shape[0] // seqs
    n = len(pieces)
    steps = GROUPS // BATCH
    wide, narrow = query.shape[1] // steps, arrays[0].shape[1] // 2 // steps
    places = [2 * steps * p[1] for p in pieces]
    head = narrow // BATCH
    biased = line is not None
    scratch = [pltpu.VMEM((BATCH, 1, 2 * tokens), f32)] * 2 + [
        pltpu.VMEM((BATCH, head, 2 * tokens), f32),
        pltpu.VMEM((BATCH, 2 * tokens, head), bf16),
    ]
    extra = []
    if biased:
        scratch.append(pltpu.VMEM((2 * BATCH, n + 1, tokens, tokens), f32))
        extra = [pl.BlockSpec((1, 2 * BATCH, line.shape[2]), lambda i, info: (i, 0, 0))]
    pairs = n * count * seqs * tokens * GROUPS * 2
    return pl.pallas_call(
        functools.partial(attend_kernel, biased, seqs, tokens, count, n, BATCH),
        grid_spec=pltpu.PrefetchScalarGridSpec(
            num_scalar_prefetch=1,
            grid=(steps,),
            in_specs=extra
            + [block_of(query, wide)]
            + [block_of(a, narrow, p) for a, p in zip(arrays, places)]
            + [block_of(a, narrow, p + steps) for a, p in zip(arrays, places)],
            out_specs=[
                block_of(query, wide),
                pl.BlockSpec((1, BATCH * seqs, 2 * tokens), lambda i, info: (i, 0, 0)),
            ],
            scratch_shapes=scratch,
        ),
        out_shape=[
            jax.ShapeDtypeStruct(query.shape, bf16),
            jax.ShapeDtypeStruct((steps, BATCH * seqs, 2 * tokens), f32),
        ],
        compiler_params=pltpu.CompilerParams(vmem_limit_bytes=40 * 1024 * 1024),
        cost_estimate=LIGHT,
    )(info, *([line] if biased else []), query, *arrays, *arrays)


def attend_back(query, mixed, upstream, logsum, pieces, info, seqs, line, after=()):
    tokens = query.shape[0] // seqs
    arrays = [p[0] for p in pieces]
    count = arrays[0].shape[0] // seqs
    n = len(pieces)
    steps = GROUPS // BATCH
    wide, narrow = query.shape[1] // steps, arrays[0].shape[1] // 2 // steps
    places = [2 * steps * p[1] for p in pieces]
    head = narrow // BATCH
    biased = line is not None
    scratch = [
        pltpu.VMEM((BATCH, head, 2 * tokens), f32),
        pltpu.VMEM((BATCH, 2 * tokens, head), bf16),
        pltpu.VMEM((BATCH, 2 * tokens, head), bf16),
        pltpu.VMEM((BATCH, 1, 2 * tokens), f32),
    ]
    extra, extra_out, extra_shape = [], [], []
    if biased:
        scratch += [pltpu.VMEM((2 * BATCH, n + 1, tokens, tokens), f32)] * 2
        extra = [pl.BlockSpec((1, 2 * BATCH, line.shape[2]), lambda i, info: (i, 0, 0))]
        extra_out = [pl.BlockSpec((1, 2 * BATCH, tokens * (n + 2)), lambda i, info: (i, 0, 0))]
        extra_shape = [jax.ShapeDtypeStruct((steps, 2 * BATCH, tokens * (n + 2)), f32)]
    part = pl.BlockSpec((n, seqs * count, narrow), lambda i, info: (0, 0, i))
    part_shape = jax.ShapeDtypeStruct((n, seqs * count, narrow * steps), bf16)
    pairs = n * count * seqs * tokens * GROUPS * 2
    return pl.pallas_call(
        functools.partial(back_kernel, biased, seqs, tokens, count, n, len(after), BATCH),
        grid_spec=pltpu.PrefetchScalarGridSpec(
            num_scalar_prefetch=1,
            grid=(steps,),
            in_specs=[pl.BlockSpec(memory_space=pl.ANY)] * len(after)
            + extra
            + [block_of(query, wide)] * 3
            + [pl.BlockSpec((1, BATCH * seqs, 2 * tokens), lambda i, info: (i, 0, 0))]
            + [block_of(a, narrow, p) for a, p in zip(arrays, places)]
            + [block_of(a, narrow, p + steps) for a, p in zip(arrays, places)],
            out_specs=[block_of(query, wide), part, part] + extra_out,
            scratch_shapes=scratch,
        ),
        out_shape=[jax.ShapeDtypeStruct(query.shape, bf16), part_shape, part_shape] + extra_shape,
        compiler_params=pltpu.CompilerParams(vmem_limit_bytes=44 * 1024 * 1024),
        cost_estimate=LIGHT,
    )(info, *after, *([line] if biased else []), query, mixed, upstream, logsum, *arrays, *arrays)


def feed_kernel(core_ref, first_ref, mixed, out_w, live, gain, grad_low, gate_w, up_w, down_w, normed, hidden, own, pair, outputs, grad, mixed_grad, gain_grad, second, result, feed_in):
    step = pl.program_id(0)

    @pl.when(step == 0)
    def _():
        value = first_ref[...] + mm(mixed[...], out_w[...])
        second[...] = value
        normed[...] = (value * norm_rate(value) * gain[...]).astype(bf16)
        result[...] = jnp.zeros(result.shape, f32)
        feed_in[...] = jnp.zeros(feed_in.shape, f32)

    gate = mm(normed[...], gate_w[...])
    upper = mm(normed[...], up_w[...])
    incoming = nt(grad_low[...], down_w[...])
    square = gate * gate
    slope = 0.7978845608028654 * 0.044715
    bend = jnp.tanh(gate * (0.7978845608028654 + slope * square))
    rise = 0.5 * (1.0 + bend)
    curve = gate * rise
    steep = rise + 0.5 * gate * (1.0 - bend * bend) * (0.7978845608028654 + 3.0 * slope * square)
    acted = (curve * upper).astype(bf16)
    gate_grad = (incoming * upper * steep).astype(bf16)
    upper_grad = (incoming * curve).astype(bf16)
    hidden[...] = acted
    first = core_ref[0] == 0
    own[...] = jnp.where(first, gate_grad, upper_grad)
    pair[...] = jnp.where(first, upper_grad, gate_grad)
    result[...] += mm(acted, down_w[...])
    feed_in[...] += nt(gate_grad, gate_w[...]) + nt(upper_grad, up_w[...])

    @pl.when(step == pl.num_programs(0) - 1)
    def _():
        value = second[...]
        outputs[...] = ((value + result[...]) * live[...]).astype(bf16)
        part, gained = norm_back(value, norm_rate(value), gain[...], feed_in[...])
        total = grad_low[...].astype(f32) + part
        grad[...] = total
        gain_grad[...] = gained
        mixed_grad[...] = nt(total.astype(bf16), out_w[...]).astype(bf16)


def feed_forward(core, first, mixed, out_weight, live, gain, grad_low, gate_weight, up_weight, down_weight, after):
    tokens, width = first.shape
    units = gate_weight.shape[1]
    whole = pl.BlockSpec((tokens, width), lambda i: (0, 0))
    line = pl.BlockSpec((1, width), lambda i: (0, 0))
    tall = pl.BlockSpec((width, TILE), lambda i: (0, i))
    part = pl.BlockSpec((tokens, TILE), lambda i: (0, i))
    part_shape = jax.ShapeDtypeStruct((tokens, units), bf16)
    low_shape = jax.ShapeDtypeStruct((tokens, width), bf16)
    skip = len(after)

    def body(core_ref, *refs):
        feed_kernel(core_ref, *refs[skip:])

    return pl.pallas_call(
        body,
        grid=(units // TILE,),
        in_specs=[pl.BlockSpec(memory_space=pltpu.SMEM)]
        + [pl.BlockSpec(memory_space=pl.ANY)] * skip
        + [
            whole,
            whole,
            pl.BlockSpec(out_weight.shape, lambda i: (0, 0)),
            pl.BlockSpec((tokens, 1), lambda i: (0, 0)),
            line,
            whole,
            tall,
            tall,
            pl.BlockSpec((TILE, width), lambda i: (i, 0)),
        ],
        out_specs=[whole, part, part, part, whole, whole, whole, line],
        out_shape=[low_shape]
        + [part_shape] * 3
        + [
            low_shape,
            jax.ShapeDtypeStruct((tokens, width), f32),
            low_shape,
            jax.ShapeDtypeStruct((1, width), f32),
        ],
        scratch_shapes=[pltpu.VMEM((tokens, width), f32)] * 3,
        compiler_params=pltpu.CompilerParams(vmem_limit_bytes=60 * 1024 * 1024),
        cost_estimate=LIGHT,
    )(core, *after, first, mixed, out_weight, live, gain.reshape(1, -1), grad_low, gate_weight, up_weight, down_weight)


def between_kernel(x, mixed, out_w, gain, query_w, first, normed, query):
    value = x[...].astype(f32) + mm(mixed[...], out_w[...])
    first[...] = value
    low = (value * norm_rate(value) * gain[...]).astype(bf16)
    normed[...] = low
    query[...] = mm(low, query_w[...]).astype(bf16)


def between_back_kernel(core_ref, query_grad, query_w, second_grad, first_ref, gain, out_w, grad, mixed_grad, own, other, gain_grad):
    value = first_ref[...]
    part, gained = norm_back(value, norm_rate(value), gain[...], nt(query_grad[...], query_w[...]))
    total = second_grad[...] + part
    grad[...] = total
    gain_grad[...] = gained
    low = total.astype(bf16)
    mixed_grad[...] = nt(low, out_w[...]).astype(bf16)
    first = core_ref[0] == 0
    half = low.shape[1] // 2
    for i, array in enumerate((second_grad[...].astype(bf16), query_grad[...], low)):
        left, right = array[:, :half], array[:, half:]
        own[:, i * half : (i + 1) * half] = jnp.where(first, left, right)
        other[:, i * half : (i + 1) * half] = jnp.where(first, right, left)


def enter_back_kernel(core_ref, query_grad, half, rest, query_w, key_w, value_w, x, gain, first_grad, grad, gain_grad):
    first = core_ref[0] == 0
    keys = jnp.where(first, half[...], rest[...])
    values = jnp.where(first, rest[...], half[...])
    incoming = nt(query_grad[...], query_w[...]) + nt(keys, key_w[...]) + nt(values, value_w[...])
    value = x[...].astype(f32)
    part, gained = norm_back(value, norm_rate(value), gain[...], incoming)
    grad[...] = first_grad[...] + part
    gain_grad[...] = gained


def whole_call(kernel, shapes, *arrays, core=None, after=()):
    vmem = pl.BlockSpec(memory_space=pltpu.VMEM)
    scalars = [] if core is None else [core]
    skip, lead = len(after), len(scalars)

    def body(*refs):
        kernel(*refs[:lead], *refs[lead + skip :])

    return pl.pallas_call(
        body,
        in_specs=[pl.BlockSpec(memory_space=pltpu.SMEM)] * lead
        + [pl.BlockSpec(memory_space=pl.ANY)] * skip
        + [vmem] * len(arrays),
        out_specs=[vmem] * len(shapes),
        out_shape=[jax.ShapeDtypeStruct(*shape) for shape in shapes],
        compiler_params=pltpu.CompilerParams(vmem_limit_bytes=32 * 1024 * 1024),
        cost_estimate=LIGHT,
    )(*scalars, *after, *arrays)


def per_device(
    inputs,
    memory,
    target_length,
    memory_length,
    distance_bucket,
    bias_table,
    self_gain,
    self_query,
    self_key,
    self_value,
    self_out,
    cross_gain,
    cross_query,
    cross_key,
    cross_value,
    cross_out,
    feed_gain,
    gate_weight,
    up_weight,
    down_weight,
    upstream,
):
    tokens, seqs, width = inputs.shape
    mem_tokens = memory.shape[0]
    size = lax.axis_size("seq")
    length = tokens * size
    buckets = bias_table.shape[0]
    me = lax.axis_index("seq")

    def flat(array):
        return jnp.transpose(array, (1, 0, 2)).reshape(-1, array.shape[2])

    def unflat(array):
        return jnp.transpose(array.reshape(seqs, -1, array.shape[1]), (1, 0, 2))

    positions = me * tokens + jnp.arange(tokens, dtype=jnp.int32)
    live = (positions[None, :] < target_length[:, None]).reshape(-1, 1)
    held = me * mem_tokens + jnp.arange(mem_tokens, dtype=jnp.int32)
    held = (held[None, :] < memory_length[:, None]).reshape(-1, 1)
    me_line = me.astype(jnp.int32).reshape(1)
    self_info = jnp.concatenate([me_line, (me * tokens < target_length).astype(jnp.int32)])
    cross_info = jnp.concatenate([me_line, (memory_length + UNIT - 1) // UNIT])

    x = flat(inputs)
    xf = x.astype(f32)
    mem = jnp.where(held, flat(memory), 0)
    grad_low = jnp.where(live, flat(upstream), 0)
    rate_self = norm_rate(xf)
    normed_self = (xf * rate_self * self_gain).astype(bf16)
    keys = mm(normed_self, self_key).astype(bf16)
    values = mm(normed_self, self_value).astype(bf16)
    held_kv = gather_start(jnp.concatenate([keys, values], axis=1))
    memory_kv = jnp.concatenate(
        [mm(mem, cross_key).astype(bf16), mm(mem, cross_value).astype(bf16)], axis=1
    )
    gathered = gather_finish(held_kv)
    held_memory = gather_start(tie([memory_kv], held_kv[1:])[0])
    query = mm(normed_self, self_query).astype(bf16)

    bucket_match = distance_bucket[:, None] == jnp.arange(buckets, dtype=jnp.int32)[None, :]
    bucket_onehot = bucket_match.astype(f32)
    line = jnp.dot(bias_table.T, bucket_onehot.T, precision=highest, preferred_element_type=f32)
    line = jnp.concatenate([jnp.full((line.shape[0], 2 * tokens), negative, f32), line], axis=1)
    line = line.reshape(GROUPS // BATCH, -1, length + 2 * tokens)

    self_mixed, self_logsum = attend(query, gathered, self_info, seqs, line)
    recalled = gather_finish(held_memory[:1] + tie(held_memory[1:], [self_mixed]))
    full, low_full, row = (x.shape, f32), (x.shape, bf16), ((1, width), f32)
    first, normed_cross, recall_query = whole_call(
        between_kernel,
        [full, low_full, (query.shape, bf16)],
        x,
        self_mixed,
        self_out,
        cross_gain.reshape(1, -1),
        cross_query,
    )
    cross_mixed, cross_logsum = attend(recall_query, recalled, cross_info, seqs, None)
    core = (me % 2).astype(jnp.int32).reshape(1)
    shared = jnp.concatenate([normed_self, self_mixed, normed_cross, cross_mixed], axis=1)
    normed_feed, hidden, gu_own, gu_other, outputs, second_grad, cross_mixed_grad, feed_gain_grad = feed_forward(
        core,
        first,
        cross_mixed,
        cross_out,
        live.astype(f32),
        feed_gain,
        grad_low,
        gate_weight,
        up_weight,
        down_weight,
        [shared],
    )
    low_own, low_pair = pair_grad(*cut(grad_low))
    mem_pair = exchange(mem, "seq", 1)
    feed_pair = exchange(normed_feed, "seq", 1)
    hidden_pair = exchange(hidden, "seq", 1)
    gu_pair = exchange(gu_other, "seq", 1)
    hidden_cols = hidden.shape[1]
    tiles = hidden_cols // TILE
    cutting = tiles // 2
    gu_task = (((0, 0), (1, 0), (2, 0), (3, 0)), width)
    feed_chain = Chain.of(
        group_grads(
            [normed_feed, feed_pair, gu_own, gu_pair, hidden, hidden_pair, low_own, low_pair],
            [
                (((4, 0), (5, 0), (6, 0), (7, 0)), hidden_cols, [(0, 0), (1, TILE)]),
                gu_task + ([(0, j * TILE) for j in range(cutting)],),
                gu_task + ([(1, j * TILE) for j in range(cutting, tiles)],),
            ],
        )
    )
    before = [feed_chain.send[0]]
    feed_first = feed_chain.start()
    recall_query_grad, memory_kept, memory_rest = attend_back(
        recall_query, cross_mixed, cross_mixed_grad, cross_logsum, recalled, cross_info, seqs, None, before
    )
    first_grad, self_mixed_grad, grads_own, grads_other, cross_gain_grad = whole_call(
        between_back_kernel,
        [full, (query.shape, bf16), ((x.shape[0], 3 * width // 2), bf16), ((x.shape[0], 3 * width // 2), bf16), row],
        recall_query_grad,
        cross_query,
        second_grad,
        first,
        cross_gain.reshape(1, -1),
        self_out,
        core=core,
    )
    query_grad, kept, rest, line_grad = attend_back(
        query, self_mixed, self_mixed_grad, self_logsum, gathered, self_info, seqs, line
    )
    grads_pair = exchange(grads_other, "seq", 1)
    shared = exchange(shared, "seq", 1)

    memory_parts = scatter_start(memory_kept, memory_rest)
    kept, rest, query_grad = tie([kept, rest, query_grad], feed_first + [grads_pair, shared])
    key_parts = scatter_start(kept, rest)
    feed_chain.add()
    feed_second = feed_chain.start([kept])
    query_own, query_other = core_halves(*cut(query_grad))
    query_pair = exchange(query_other, "seq", 1)
    two = [(0, 0), (1, TILE)]
    out_chain = Chain.of(
        group_grads(
            [cross_mixed, normed_cross, self_mixed, shared, grads_own, grads_pair],
            [
                (((0, 0), (3, 3 * width), (4, 0), (5, 0)), width, two),
                (((1, 0), (3, 2 * width), (4, width // 2), (5, width // 2)), width, two),
                (((2, 0), (3, width), (4, width), (5, width)), width, two),
            ],
            [query_grad],
        )
    )
    line_grad = line_grad.reshape(-1, line_grad.shape[2])[:, 2 * tokens :]
    table_grad = jnp.dot(line_grad, bucket_onehot, precision=highest, preferred_element_type=f32).T
    arrived = feed_second + memory_parts[1:] + key_parts[1:] + [query_pair, out_chain.send[0]]

    key_sent = scatter_send(key_parts[:1] + tie(key_parts[1:], arrived))
    memory_sent = scatter_send(memory_parts[:1] + tie(memory_parts[1:], arrived))
    feed_chain.add()
    feed_chain.to_dp()
    feed_chain = Chain.merged([feed_chain])
    feed_z = feed_chain.start(arrived)
    key_half, key_half_pair, key_other = scatter_finish(key_parts[0], key_sent)
    memory_half, memory_half_pair, memory_other = scatter_finish(memory_parts[0], memory_sent)
    arrived = key_sent + memory_sent + feed_z

    out_first = out_chain.start(arrived)
    feed_chain.add()
    feed_z = feed_chain.start(arrived)
    in_chain = Chain.of(
        group_grads(
            [normed_self, shared, query_own, query_pair, key_half, key_half_pair, mem, mem_pair, memory_half, memory_half_pair],
            [
                (((6, 0), (7, 0), (8, 0), (9, 0)), width, two),
                (((0, 0), (1, 0), (2, 0), (3, 0)), width, two),
                (((0, 0), (1, 0), (4, 0), (5, 0)), width, two),
            ],
            arrived,
        )
    )
    in_first = in_chain.start()
    memory_key_low, memory_value_low = core_halves(memory_half, memory_other)
    memory_grad = mm_t(memory_key_low, cross_key) + mm_t(memory_value_low, cross_value)
    input_grad, self_gain_grad = whole_call(
        enter_back_kernel,
        [full, row],
        query_grad,
        key_half,
        key_other,
        self_query,
        self_key,
        self_value,
        x,
        self_gain.reshape(1, -1),
        first_grad,
        core=core,
        after=[in_chain.send[0]],
    )
    small = jnp.concatenate(
        [v.reshape(-1) for v in (self_gain_grad, cross_gain_grad, feed_gain_grad, table_grad)]
    ).reshape(-1, 128)
    small = sum_over(small, [("seq", 1)])
    arrived = in_first + out_first + feed_z + [small]

    dp_bits, seq_bits = bits_of(lax.axis_size("dp"), 1), bits_of(lax.axis_size("seq"), 2)
    small = sum_over(tie([small], arrived)[0], [("dp", bit) for bit in dp_bits[:1]])
    in_chain.add()
    out_chain.add()
    in_second = in_chain.start(arrived)
    out_second = out_chain.start(arrived)
    feed_chain.add()
    arrived = in_second + out_second + [small]

    out_chain.add()
    in_chain.add()
    out_chain.to_dp()
    in_chain.to_dp()
    last_chain = Chain.merged([out_chain, in_chain])
    last_z = last_chain.start(arrived)
    small = sum_over(tie([small], arrived)[0], [("dp", bit) for bit in dp_bits[1:]])
    small = sum_over(small, [("seq", bit) for bit in seq_bits]).reshape(-1)
    last_chain.add()

    blocks = 2 ** len(grad_order(False))
    narrow, broad = width // blocks, hidden_cols // blocks
    piece = feed_chain.finish()
    middle = broad + cutting * narrow
    gate_up = jnp.concatenate([piece[broad:middle], piece[middle + broad :]], axis=0)
    down = jnp.concatenate([piece[:broad], piece[middle : middle + broad]], axis=0)
    (gate_out, up_out), down_out = swap_rows(
        [gate_up.reshape(tiles, narrow, TILE), down.reshape(2, broad, TILE)]
    )
    piece = last_chain.finish().reshape(-1, narrow, TILE)
    outs, ins = piece[:6].reshape(2, 3, narrow, TILE), piece[6:].reshape(2, 3, narrow, TILE)
    cross_out_out, cross_query_out, self_out_out, cross_kv_out, self_query_out, self_kv_out = swap_rows(
        [outs[:, i] for i in range(3)] + [ins[:, i] for i in range(3)]
    )

    def joined(pair):
        return jnp.concatenate(pair, axis=1)

    return (
        unflat(outputs),
        unflat(input_grad),
        unflat(memory_grad),
        small[:width],
        joined(self_query_out),
        self_kv_out[0],
        self_kv_out[1],
        joined(self_out_out),
        small[3 * width :].reshape(buckets, -1),
        small[width : 2 * width],
        joined(cross_query_out),
        cross_kv_out[0],
        cross_kv_out[1],
        joined(cross_out_out),
        small[2 * width : 3 * width],
        gate_out,
        up_out,
        joined(down_out),
    )


def solution(mesh):
    placed = P("seq", "dp", None)
    rows = P(("dp", "seq"), None)
    return jax.shard_map(
        per_device,
        mesh=mesh,
        in_specs=(placed, placed, P("dp"), P("dp")) + (P(),) * 16 + (placed,),
        out_specs=(
            placed,
            placed,
            placed,
            P(),
            rows,
            rows,
            rows,
            rows,
            P(),
            P(),
            rows,
            rows,
            rows,
            rows,
            P(),
            rows,
            rows,
            rows,
        ),
        check_vma=False,
    )
```

```python
import functools

import jax
import jax.numpy as jnp
from jax import lax
from jax.experimental import pallas as pl
from jax.experimental.pallas import tpu as pltpu
from jax.sharding import PartitionSpec as P

GROUPS = 8


epsilon = 1e-06
scale = 0.125
negative = -1e30
highest = lax.Precision.HIGHEST
bf16 = jnp.bfloat16
f32 = jnp.float32


def norm_rate(value):
    return lax.rsqrt(jnp.mean(value * value, axis=-1, keepdims=True) + epsilon)


def norm_back(value, rate, gain, incoming):
    scaled = incoming * gain
    inner = jnp.mean(scaled * value, axis=-1, keepdims=True)
    grad = rate * (scaled - value * (rate * rate * inner))
    return grad, jnp.sum(incoming * value * rate, axis=0, keepdims=True)


def mm(left, right):
    return jnp.dot(left, right, preferred_element_type=f32)


def mm_t(grad, weight):
    return lax.dot_general(grad, weight, (((1,), (1,)), ((), ())), preferred_element_type=f32)


def exchange(value, axis, bit):
    size = lax.axis_size(axis)
    return lax.ppermute(value, axis, [(i, i ^ bit) for i in range(size)])


def bits_of(size, lowest):
    bits = []
    bit = lowest
    while bit < size:
        bits.append(bit)
        bit = bit * 2
    return bits


TILE = 256
LIGHT = pl.CostEstimate(flops=1, bytes_accessed=1, transcendentals=0)


def grad_order(flip):
    seq_bits = bits_of(lax.axis_size("seq"), 2)
    if flip:
        seq_bits = seq_bits[::-1]
    return [("seq", b) for b in seq_bits] + [("dp", b) for b in bits_of(lax.axis_size("dp"), 1)]


def grads_kernel(chips, orders, tasks, sources, count, me_ref, *refs):
    ins, refs = refs[:sources], refs[count:]
    outs, (turned, total) = refs[:4], refs[4:]
    blocks = 2 ** len(orders[0])
    filled = [0, 0]
    for (xo, xp, do, dp), tokens, rows, rchip, tiles in tasks:
        for half, (place, lane) in enumerate((xo, xp)):
            turned[:rows, half * tokens : (half + 1) * tokens] = ins[place][:, lane : lane + rows].T
        for stack, lane in tiles:
            value = mm(turned[:rows, :tokens], ins[do[0]][:, do[1] + lane : do[1] + lane + TILE])
            value = value + mm(
                turned[:rows, tokens : 2 * tokens], ins[dp[0]][:, dp[1] + lane : dp[1] + lane + TILE]
            )
            for block in range(blocks):
                total[block, :rchip] = value[block * rchip : (block + 1) * rchip]
            order = orders[stack]
            for slot in range(blocks):
                seq_part, dp_part = 0, 0
                for place, (axis, bit) in enumerate(order):
                    if (slot >> (len(order) - 1 - place)) & 1:
                        if axis == "seq":
                            seq_part = seq_part | (bit // 2)
                        else:
                            dp_part = dp_part | bit
                block = (me_ref[0] ^ dp_part) * chips + (me_ref[1] ^ seq_part)
                outs[2 * stack + slot // (blocks // 2)][
                    slot % (blocks // 2), filled[stack] : filled[stack] + rchip
                ] = total[block, :rchip].astype(bf16)
            filled[stack] += rchip


def block_whole(array):
    return pl.BlockSpec(array.shape, lambda i: (0,) * len(array.shape))


def group_grads(arrays, tasks, after=()):
    chips = lax.axis_size("seq") // 2
    orders = [grad_order(False), grad_order(True)]
    blocks = 2 ** len(orders[0])
    full = []
    depth = [0, 0]
    flops = 0
    for names, rows, tiles in tasks:
        tokens = arrays[names[0][0]].shape[0]
        full.append((names, tokens, rows, rows // blocks, tiles))
        flops += 4 * tokens * rows * TILE * len(tiles)
        for stack, lane in tiles:
            depth[stack] += rows // blocks
    me = jnp.stack([lax.axis_index("dp"), lax.axis_index("seq") // 2]).astype(jnp.int32)
    most = max(t[2] for t in full)
    shapes = [jax.ShapeDtypeStruct((blocks // 2, depth[i // 2], TILE), bf16) for i in range(4)]
    total = arrays[0].dtype.itemsize * sum(a.size for a in arrays)
    return pl.pallas_call(
        functools.partial(grads_kernel, chips, orders, full, len(arrays), len(arrays) + len(after)),
        grid=(1,),
        in_specs=[pl.BlockSpec(memory_space=pltpu.SMEM)]
        + [block_whole(a) for a in arrays]
        + [pl.BlockSpec(memory_space=pl.ANY)] * len(after),
        out_specs=[block_whole(a) for a in shapes],
        scratch_shapes=[
            pltpu.VMEM((most, max(2 * t[1] for t in full)), bf16),
            pltpu.VMEM((blocks, most // blocks, TILE), f32),
        ],
        out_shape=shapes,
        compiler_params=pltpu.CompilerParams(vmem_limit_bytes=60 * 1024 * 1024),
        cost_estimate=LIGHT,
    )(me, *arrays, *after)


class Chain:
    def __init__(self, keep, send, orders, level=0):
        self.keep, self.send, self.orders, self.level, self.got = keep, send, orders, level, None

    @staticmethod
    def of(outs):
        return Chain([outs[0], outs[2]], [outs[1], outs[3]], [grad_order(False), grad_order(True)])

    @staticmethod
    def merged(chains):
        level = chains[0].level
        if chains[0].orders[0][level][0] == "dp":
            keeps = [[k for c in chains for k in c.keep]]
            sends = [[v for c in chains for v in c.send]]
        else:
            keeps = [list(k) for k in zip(*[c.keep for c in chains])]
            sends = [list(v) for v in zip(*[c.send for c in chains])]
        joined = [[jnp.concatenate(v, axis=1) for v in group] for group in (keeps, sends)]
        return Chain(joined[0], joined[1], chains[0].orders[: len(keeps)], level)

    def start(self, tokens=()):
        if tokens:
            self.send = tie(self.send, tokens)
        self.got = [exchange(v, *self.orders[i][self.level]) for i, v in enumerate(self.send)]
        self.level += 1
        return self.got

    def add(self):
        got, self.got = self.got, None
        half = got[0].shape[0] // 2
        if half:
            self.send = [k[half:] + g[half:] for k, g in zip(self.keep, got)]
            self.keep = [k[:half] + g[:half] for k, g in zip(self.keep, got)]
        else:
            self.keep = [k.astype(f32) + g.astype(f32) for k, g in zip(self.keep, got)]

    def to_dp(self):
        while self.orders[0][self.level][0] == "seq":
            self.start()
            self.add()

    def last(self):
        while self.level < len(self.orders[0]):
            if self.got is not None:
                self.add()
            self.start()
        return self.keep[0], self.got[0]


def split_kernel(tiles, core_ref, keep, got, mine, other):
    first = core_ref[0] == 0
    start = 0
    for row, rows in tiles:
        half = rows // 2
        value = keep[0, row : row + rows].astype(f32) + got[0, row : row + rows].astype(f32)
        low, high = value[:half], value[half:]
        mine[start : start + half] = jnp.where(first, low, high)
        other[start : start + half] = jnp.where(first, high, low).astype(bf16)
        start += half


def place_kernel(weights, core_ref, mine, got, *outs):
    first = core_ref[0] == 0
    for tiles, half, (left, shift_left), (right, shift_right) in weights:
        for i, row in enumerate(tiles):
            own, swapped = mine[row : row + half], got[row : row + half].astype(f32)
            outs[left][:, shift_left + i * TILE : shift_left + (i + 1) * TILE] = jnp.where(first, own, swapped)
            outs[right][:, shift_right + i * TILE : shift_right + (i + 1) * TILE] = jnp.where(first, swapped, own)


def finish_rows(core, keep, got, tiles, weights, after=()):
    starts, total = [], 0
    listed = []
    for rows in tiles:
        listed.append((2 * total, rows))
        starts.append(total)
        total += rows // 2
    mine, other = whole_call(
        functools.partial(split_kernel, listed), [((total, TILE), f32), ((total, TILE), bf16)], keep, got, core=core, after=after
    )
    arrived = exchange(other, "seq", 1)
    shapes, plan = [], []
    for places, joined in weights:
        half, columns = tiles[places[0]] // 2, len(places) * TILE
        rows = [starts[p] for p in places]
        if joined:
            plan.append((rows, half, (len(shapes), 0), (len(shapes), columns)))
            shapes.append(((half, 2 * columns), f32))
        else:
            plan.append((rows, half, (len(shapes), 0), (len(shapes) + 1, 0)))
            shapes += [((half, columns), f32)] * 2
    return whole_call(functools.partial(place_kernel, plan), shapes, mine, arrived, core=core)


def core_halves(left, right):
    core = lax.axis_index("seq") % 2
    return jnp.where(core == 0, left, right), jnp.where(core == 0, right, left)


def pair_grad(left, right):
    mine, other = core_halves(left, right)
    return mine, exchange(other, "seq", 1)


def cut(value):
    half = value.shape[1] // 2
    return value[:, :half], value[:, half:]


def tie(values, tokens):
    done = lax.optimization_barrier((tuple(values), tuple(tokens)))
    return list(done[0])


def gather_start(value):
    chips = lax.axis_size("seq") // 2
    return [value] + [exchange(value, "seq", 2 * chip) for chip in range(1, chips)]


def gather_finish(mine):
    own = exchange(mine[0], "seq", 1)
    rest = exchange(jnp.concatenate(mine[1:], axis=1), "seq", 1)
    pieces = []
    for chip, value in enumerate(mine):
        pieces.append((value, 0))
        pieces.append((own, 0) if chip == 0 else (rest, chip - 1))
    return pieces


def scatter_start(mine, other):
    got = exchange(other, "seq", 1)
    parts = []
    for chip in range(mine.shape[0] // 2):
        pair = slice(2 * chip, 2 * chip + 2)
        part = mine[pair].astype(f32) + got[pair].astype(f32)
        parts.append(part if chip == 0 else part.astype(bf16))
    return parts


def scatter_send(parts):
    return [exchange(part, "seq", 2 * (chip + 1)) for chip, part in enumerate(parts[1:])]


def scatter_finish(part, arrived):
    total = part
    for value in arrived:
        total = total + value.astype(f32)
    total = total.astype(bf16)
    return total[0], total[1]


def sum_over(value, steps):
    for axis, bit in steps:
        value = value + exchange(value, axis, bit)
    return value


UNIT = 256


def nt(left, right):
    return lax.dot_general(left, right, (((1,), (1,)), ((), ())), preferred_element_type=f32)


def make_strip(e_ref, strip, tokens):
    heads, parts = strip.shape[0], strip.shape[1]
    for h in range(heads):
        line = e_ref[0, h : h + 1, :]
        turned = pltpu.roll(
            jnp.broadcast_to(line, (tokens, line.shape[1])), 0, 1, stride=1, stride_axis=0
        )
        for d in range(parts):
            strip[h, d] = turned[:, tokens * (d + 1) : tokens * (d + 2)]


def two_heads(ref, rows, lane, head):
    return jnp.concatenate(
        [ref[rows, lane : lane + head], ref[rows, lane + head : lane + 2 * head]], axis=0
    )


def unit_rows(refs, unit, per_unit, count, s, lane, head):
    return jnp.concatenate(
        [
            refs[unit * per_unit + p][s * count : (s + 1) * count, lane : lane + head]
            for p in range(per_unit)
        ],
        axis=0,
    )


def unit_bias(strip, me, unit, per_unit, group):
    rows = []
    for p in range(per_unit):
        place = me - (me ^ (unit * per_unit + p)) + 1
        rows.append(jnp.concatenate([strip[2 * group, place], strip[2 * group + 1, place]], axis=1))
    return jnp.concatenate(rows, axis=0)


def attend_kernel(biased, seqs, tokens, count, pieces, batch, *refs):
    info, refs = refs[0], refs[1:]
    if biased:
        e_ref, refs = refs[0], refs[1:]
    q_ref, refs = refs[0], refs[1:]
    k_refs, v_refs = refs[:pieces], refs[pieces : 2 * pieces]
    out_ref, lse_ref, peak, total, mixed, queries = refs[2 * pieces : 2 * pieces + 6]
    if biased:
        strip = refs[2 * pieces + 6]
        make_strip(e_ref, strip, tokens)
    per_unit = UNIT // count
    units = pieces // per_unit
    me = info[0]
    mine = me // per_unit
    head = q_ref.shape[1] // (2 * batch)
    for s in range(seqs):
        rows = slice(s * tokens, (s + 1) * tokens)

        @pl.when(info[1 + s] > 0)
        def _(s=s, rows=rows):
            for g in range(batch):
                queries[g] = two_heads(q_ref, rows, 2 * g * head, head) * scale
            peak[...] = jnp.full(peak.shape, -3e38, f32)
            total[...] = jnp.zeros(total.shape, f32)
            mixed[...] = jnp.zeros(mixed.shape, f32)
            for unit in range(units):
                if biased:
                    used = (unit ^ mine) <= mine
                else:
                    used = (unit ^ mine) < info[1 + s]

                @pl.when(used)
                def _(unit=unit):
                    states = []
                    for g in range(batch):
                        k = unit_rows(k_refs, unit, per_unit, count, s, g * head, head)
                        scores = nt(k, queries[g])
                        if biased:
                            scores = scores + unit_bias(strip, me, unit, per_unit, g)
                        states.append((scores, peak[g], total[g], mixed[g]))
                    done = []
                    for g, (scores, old, summed, part) in enumerate(states):
                        v = unit_rows(v_refs, unit, per_unit, count, s, g * head, head)
                        top = jnp.maximum(old, jnp.max(scores, axis=0, keepdims=True))
                        raised = jnp.exp(scores - top)
                        fade = jnp.exp(old - top)
                        done.append(
                            (
                                top,
                                summed * fade + jnp.sum(raised, axis=0, keepdims=True),
                                part * fade + mm(v.T, raised.astype(bf16)),
                            )
                        )
                    for g in range(batch):
                        peak[g], total[g], mixed[g] = done[g]

            for g in range(batch):
                lse_ref[0, batch * s + g : batch * s + g + 1, :] = peak[g] + jnp.log(total[g])
                done = (mixed[g] / total[g]).T.astype(bf16)
                out_ref[rows, 2 * g * head : 2 * (g + 1) * head] = jnp.concatenate(
                    [done[:tokens], done[tokens:]], axis=1
                )

        @pl.when(info[1 + s] <= 0)
        def _(s=s, rows=rows):
            lse_ref[0, batch * s : batch * (s + 1), :] = jnp.zeros((batch, 2 * tokens), f32)
            out_ref[rows, :] = jnp.zeros((tokens, out_ref.shape[1]), bf16)


def back_kernel(biased, seqs, tokens, count, pieces, after, batch, *refs):
    info, refs = refs[0], refs[1 + after :]
    if biased:
        e_ref, refs = refs[0], refs[1:]
    q_ref, o_ref, do_ref, lse_ref, refs = refs[0], refs[1], refs[2], refs[3], refs[4:]
    k_refs, v_refs, refs = refs[:pieces], refs[pieces : 2 * pieces], refs[2 * pieces :]
    dq_ref, keep, send, refs = refs[0], refs[1], refs[2], refs[3:]
    if biased:
        table_ref, refs = refs[0], refs[1:]
    dq, queries, grads, inner = refs[:4]
    if biased:
        strip, sums = refs[4:]
        make_strip(e_ref, strip, tokens)
        sums[...] = jnp.zeros(sums.shape, f32)
    per_unit = UNIT // count
    units = pieces // per_unit
    me = info[0]
    mine = me // per_unit
    first = me % 2 == 0
    head = q_ref.shape[1] // (2 * batch)
    for s in range(seqs):
        rows = slice(s * tokens, (s + 1) * tokens)
        keys = slice(s * count, (s + 1) * count)

        def clear(unit, keys=keys):
            for p in range(per_unit):
                piece = unit * per_unit + p
                keep[piece, keys, :] = jnp.zeros((count, batch * head), bf16)
                send[piece ^ 1, keys, :] = jnp.zeros((count, batch * head), bf16)

        @pl.when(info[1 + s] > 0)
        def _(s=s, rows=rows, keys=keys, clear=clear):
            for g in range(batch):
                lane = 2 * g * head
                queries[g] = two_heads(q_ref, rows, lane, head) * scale
                do2 = two_heads(do_ref, rows, lane, head)
                o2 = two_heads(o_ref, rows, lane, head)
                grads[g] = do2
                inner[g] = jnp.sum((o2.astype(f32) * do2.astype(f32)).T, axis=0, keepdims=True)
            dq[...] = jnp.zeros(dq.shape, f32)
            for unit in range(units):
                if biased:
                    used = (unit ^ mine) <= mine
                else:
                    used = (unit ^ mine) < info[1 + s]

                @pl.when(used)
                def _(unit=unit):
                    states = []
                    for g in range(batch):
                        k = unit_rows(k_refs, unit, per_unit, count, s, g * head, head)
                        v = unit_rows(v_refs, unit, per_unit, count, s, g * head, head)
                        scores = nt(k, queries[g])
                        if biased:
                            scores = scores + unit_bias(strip, me, unit, per_unit, g)
                        states.append((k, scores, nt(v, grads[g])))
                    done, turned = [], []
                    for g, (k, scores, down) in enumerate(states):
                        share = jnp.exp(scores - lse_ref[0, batch * s + g : batch * s + g + 1, :])
                        grad = (share * (down - inner[g])).astype(bf16)
                        dv = mm(share.astype(bf16), grads[g])
                        dk = mm(grad, queries[g])
                        turned.append(mm(k.T, grad))
                        done.append(
                            (
                                grad,
                                jnp.where(first, dk, dv).astype(bf16),
                                jnp.where(first, dv, dk).astype(bf16),
                            )
                        )
                    for g in range(batch):
                        dq[g] += turned[g]
                    kept = jnp.concatenate([d[1] for d in done], axis=1)
                    sent = jnp.concatenate([d[2] for d in done], axis=1)
                    for p in range(per_unit):
                        piece = unit * per_unit + p
                        part = slice(p * count, (p + 1) * count)
                        keep[piece, keys, :] = kept[part]
                        send[piece ^ 1, keys, :] = sent[part]
                        if biased:
                            place = me - (me ^ piece) + 1
                            for g in range(batch):
                                for h in range(2):
                                    sums[2 * g + h, place] += done[g][0][
                                        part, h * tokens : (h + 1) * tokens
                                    ].astype(f32)

                @pl.when(jnp.logical_not(used))
                def _(unit=unit):
                    clear(unit)

            for g in range(batch):
                done = (dq[g] * scale).T.astype(bf16)
                dq_ref[rows, 2 * g * head : 2 * (g + 1) * head] = jnp.concatenate(
                    [done[:tokens], done[tokens:]], axis=1
                )

        @pl.when(info[1 + s] <= 0)
        def _(rows=rows, clear=clear):
            for unit in range(units):
                clear(unit)
            dq_ref[rows, :] = jnp.zeros((tokens, dq_ref.shape[1]), bf16)

    if biased:
        parts = sums.shape[1]
        span = tokens * (parts + 1)
        for h in range(2 * batch):
            line = jnp.concatenate(
                [jnp.zeros((tokens, tokens), f32)] + [sums[h, d] for d in range(parts)], axis=1
            )
            height = tokens
            while height > 8:
                height = height // 2
                line = line[:height] + pltpu.roll(line[height:], span - height, 1)
            while height > 1:
                height = height // 2
                upper = pltpu.roll(line, span - height, 1)
                line = line[:height] + upper[height : 2 * height]
            table_ref[0, h : h + 1, :] = line


def block_of(array, lanes, offset=0):
    return pl.BlockSpec((array.shape[0], lanes), lambda i, info: (0, offset + i))


BATCH = 4


def attend(query, pieces, info, seqs, line):
    tokens = query.shape[0] // seqs
    arrays = [p[0] for p in pieces]
    count = arrays[0].shape[0] // seqs
    n = len(pieces)
    steps = GROUPS // BATCH
    wide, narrow = query.shape[1] // steps, arrays[0].shape[1] // 2 // steps
    places = [2 * steps * p[1] for p in pieces]
    head = narrow // BATCH
    biased = line is not None
    scratch = [pltpu.VMEM((BATCH, 1, 2 * tokens), f32)] * 2 + [
        pltpu.VMEM((BATCH, head, 2 * tokens), f32),
        pltpu.VMEM((BATCH, 2 * tokens, head), bf16),
    ]
    extra = []
    if biased:
        scratch.append(pltpu.VMEM((2 * BATCH, n + 1, tokens, tokens), f32))
        extra = [pl.BlockSpec((1, 2 * BATCH, line.shape[2]), lambda i, info: (i, 0, 0))]
    pairs = n * count * seqs * tokens * GROUPS * 2
    return pl.pallas_call(
        functools.partial(attend_kernel, biased, seqs, tokens, count, n, BATCH),
        grid_spec=pltpu.PrefetchScalarGridSpec(
            num_scalar_prefetch=1,
            grid=(steps,),
            in_specs=extra
            + [block_of(query, wide)]
            + [block_of(a, narrow, p) for a, p in zip(arrays, places)]
            + [block_of(a, narrow, p + steps) for a, p in zip(arrays, places)],
            out_specs=[
                block_of(query, wide),
                pl.BlockSpec((1, BATCH * seqs, 2 * tokens), lambda i, info: (i, 0, 0)),
            ],
            scratch_shapes=scratch,
        ),
        out_shape=[
            jax.ShapeDtypeStruct(query.shape, bf16),
            jax.ShapeDtypeStruct((steps, BATCH * seqs, 2 * tokens), f32),
        ],
        compiler_params=pltpu.CompilerParams(vmem_limit_bytes=40 * 1024 * 1024),
        cost_estimate=pl.CostEstimate(flops=4096 * pairs, bytes_accessed=8 * query.size, transcendentals=pairs),
    )(info, *([line] if biased else []), query, *arrays, *arrays)


def attend_back(query, mixed, upstream, logsum, pieces, info, seqs, line, after=()):
    tokens = query.shape[0] // seqs
    arrays = [p[0] for p in pieces]
    count = arrays[0].shape[0] // seqs
    n = len(pieces)
    steps = GROUPS // BATCH
    wide, narrow = query.shape[1] // steps, arrays[0].shape[1] // 2 // steps
    places = [2 * steps * p[1] for p in pieces]
    head = narrow // BATCH
    biased = line is not None
    scratch = [
        pltpu.VMEM((BATCH, head, 2 * tokens), f32),
        pltpu.VMEM((BATCH, 2 * tokens, head), bf16),
        pltpu.VMEM((BATCH, 2 * tokens, head), bf16),
        pltpu.VMEM((BATCH, 1, 2 * tokens), f32),
    ]
    extra, extra_out, extra_shape = [], [], []
    if biased:
        scratch += [pltpu.VMEM((2 * BATCH, n + 1, tokens, tokens), f32)] * 2
        extra = [pl.BlockSpec((1, 2 * BATCH, line.shape[2]), lambda i, info: (i, 0, 0))]
        extra_out = [pl.BlockSpec((1, 2 * BATCH, tokens * (n + 2)), lambda i, info: (i, 0, 0))]
        extra_shape = [jax.ShapeDtypeStruct((steps, 2 * BATCH, tokens * (n + 2)), f32)]
    part = pl.BlockSpec((n, seqs * count, narrow), lambda i, info: (0, 0, i))
    part_shape = jax.ShapeDtypeStruct((n, seqs * count, narrow * steps), bf16)
    pairs = n * count * seqs * tokens * GROUPS * 2
    return pl.pallas_call(
        functools.partial(back_kernel, biased, seqs, tokens, count, n, len(after), BATCH),
        grid_spec=pltpu.PrefetchScalarGridSpec(
            num_scalar_prefetch=1,
            grid=(steps,),
            in_specs=[pl.BlockSpec(memory_space=pl.ANY)] * len(after)
            + extra
            + [block_of(query, wide)] * 3
            + [pl.BlockSpec((1, BATCH * seqs, 2 * tokens), lambda i, info: (i, 0, 0))]
            + [block_of(a, narrow, p) for a, p in zip(arrays, places)]
            + [block_of(a, narrow, p + steps) for a, p in zip(arrays, places)],
            out_specs=[block_of(query, wide), part, part] + extra_out,
            scratch_shapes=scratch,
        ),
        out_shape=[jax.ShapeDtypeStruct(query.shape, bf16), part_shape, part_shape] + extra_shape,
        compiler_params=pltpu.CompilerParams(vmem_limit_bytes=44 * 1024 * 1024),
        cost_estimate=LIGHT,
    )(info, *after, *([line] if biased else []), query, mixed, upstream, logsum, *arrays, *arrays)


def feed_kernel(core_ref, first_ref, mixed, out_w, live, gain, grad_low, gate_w, up_w, down_w, normed, hidden, own, pair, outputs, grad, mixed_grad, gain_grad, second, result, feed_in):
    step = pl.program_id(0)

    @pl.when(step == 0)
    def _():
        value = first_ref[...] + mm(mixed[...], out_w[...])
        second[...] = value
        normed[...] = (value * norm_rate(value) * gain[...]).astype(bf16)
        result[...] = jnp.zeros(result.shape, f32)
        feed_in[...] = jnp.zeros(feed_in.shape, f32)

    gate = mm(normed[...], gate_w[...])
    upper = mm(normed[...], up_w[...])
    incoming = nt(grad_low[...], down_w[...])
    square = gate * gate
    slope = 0.7978845608028654 * 0.044715
    bend = jnp.tanh(gate * (0.7978845608028654 + slope * square))
    rise = 0.5 * (1.0 + bend)
    curve = gate * rise
    steep = rise + 0.5 * gate * (1.0 - bend * bend) * (0.7978845608028654 + 3.0 * slope * square)
    acted = (curve * upper).astype(bf16)
    gate_grad = (incoming * upper * steep).astype(bf16)
    upper_grad = (incoming * curve).astype(bf16)
    hidden[...] = acted
    first = core_ref[0] == 0
    own[...] = jnp.where(first, gate_grad, upper_grad)
    pair[...] = jnp.where(first, upper_grad, gate_grad)
    result[...] += mm(acted, down_w[...])
    feed_in[...] += nt(gate_grad, gate_w[...]) + nt(upper_grad, up_w[...])

    @pl.when(step == pl.num_programs(0) - 1)
    def _():
        value = second[...]
        outputs[...] = ((value + result[...]) * live[...]).astype(bf16)
        part, gained = norm_back(value, norm_rate(value), gain[...], feed_in[...])
        total = grad_low[...].astype(f32) + part
        grad[...] = total
        gain_grad[...] = gained
        mixed_grad[...] = nt(total.astype(bf16), out_w[...]).astype(bf16)


def feed_forward(core, first, mixed, out_weight, live, gain, grad_low, gate_weight, up_weight, down_weight, after):
    tokens, width = first.shape
    units = gate_weight.shape[1]
    whole = pl.BlockSpec((tokens, width), lambda i: (0, 0))
    line = pl.BlockSpec((1, width), lambda i: (0, 0))
    tall = pl.BlockSpec((width, TILE), lambda i: (0, i))
    part = pl.BlockSpec((tokens, TILE), lambda i: (0, i))
    part_shape = jax.ShapeDtypeStruct((tokens, units), bf16)
    low_shape = jax.ShapeDtypeStruct((tokens, width), bf16)
    skip = len(after)

    def body(core_ref, *refs):
        feed_kernel(core_ref, *refs[skip:])

    return pl.pallas_call(
        body,
        grid=(units // TILE,),
        in_specs=[pl.BlockSpec(memory_space=pltpu.SMEM)]
        + [pl.BlockSpec(memory_space=pl.ANY)] * skip
        + [
            whole,
            whole,
            pl.BlockSpec(out_weight.shape, lambda i: (0, 0)),
            pl.BlockSpec((tokens, 1), lambda i: (0, 0)),
            line,
            whole,
            tall,
            tall,
            pl.BlockSpec((TILE, width), lambda i: (i, 0)),
        ],
        out_specs=[whole, part, part, part, whole, whole, whole, line],
        out_shape=[low_shape]
        + [part_shape] * 3
        + [
            low_shape,
            jax.ShapeDtypeStruct((tokens, width), f32),
            low_shape,
            jax.ShapeDtypeStruct((1, width), f32),
        ],
        scratch_shapes=[pltpu.VMEM((tokens, width), f32)] * 3,
        compiler_params=pltpu.CompilerParams(vmem_limit_bytes=60 * 1024 * 1024),
        cost_estimate=pl.CostEstimate(
            flops=12 * tokens * width * units, bytes_accessed=6 * width * units, transcendentals=tokens * units
        ),
    )(core, *after, first, mixed, out_weight, live, gain.reshape(1, -1), grad_low, gate_weight, up_weight, down_weight)


def between_kernel(x, mixed, out_w, gain, query_w, first, normed, query):
    value = x[...].astype(f32) + mm(mixed[...], out_w[...])
    first[...] = value
    low = (value * norm_rate(value) * gain[...]).astype(bf16)
    normed[...] = low
    query[...] = mm(low, query_w[...]).astype(bf16)


def between_back_kernel(core_ref, query_grad, query_w, second_grad, first_ref, gain, out_w, grad, mixed_grad, own, other, gain_grad):
    value = first_ref[...]
    part, gained = norm_back(value, norm_rate(value), gain[...], nt(query_grad[...], query_w[...]))
    total = second_grad[...] + part
    grad[...] = total
    gain_grad[...] = gained
    low = total.astype(bf16)
    mixed_grad[...] = nt(low, out_w[...]).astype(bf16)
    first = core_ref[0] == 0
    half = low.shape[1] // 2
    for i, array in enumerate((second_grad[...].astype(bf16), query_grad[...], low)):
        left, right = array[:, :half], array[:, half:]
        own[:, i * half : (i + 1) * half] = jnp.where(first, left, right)
        other[:, i * half : (i + 1) * half] = jnp.where(first, right, left)


def enter_back_kernel(core_ref, query_grad, half, rest, query_w, key_w, value_w, x, gain, first_grad, grad, gain_grad):
    first = core_ref[0] == 0
    keys = jnp.where(first, half[...], rest[...])
    values = jnp.where(first, rest[...], half[...])
    incoming = nt(query_grad[...], query_w[...]) + nt(keys, key_w[...]) + nt(values, value_w[...])
    value = x[...].astype(f32)
    part, gained = norm_back(value, norm_rate(value), gain[...], incoming)
    grad[...] = first_grad[...] + part
    gain_grad[...] = gained


def whole_call(kernel, shapes, *arrays, core=None, after=(), stream=False):
    vmem = pl.BlockSpec(memory_space=pltpu.VMEM)
    scalars = [] if core is None else [core]
    skip, lead = len(after), len(scalars)

    def body(*refs):
        kernel(*refs[:lead], *refs[lead + skip :])

    grid, spec, limit = {}, lambda array: vmem, 32
    if stream:
        grid, spec, limit = {"grid": (1,)}, block_whole, 60
    outs = [jax.ShapeDtypeStruct(*shape) for shape in shapes]
    return pl.pallas_call(
        body,
        **grid,
        in_specs=[pl.BlockSpec(memory_space=pltpu.SMEM)] * lead
        + [pl.BlockSpec(memory_space=pl.ANY)] * skip
        + [spec(a) for a in arrays],
        out_specs=[spec(a) for a in outs],
        out_shape=outs,
        compiler_params=pltpu.CompilerParams(vmem_limit_bytes=limit * 1024 * 1024),
        cost_estimate=LIGHT,
    )(*scalars, *after, *arrays)


def per_device(
    inputs,
    memory,
    target_length,
    memory_length,
    distance_bucket,
    bias_table,
    self_gain,
    self_query,
    self_key,
    self_value,
    self_out,
    cross_gain,
    cross_query,
    cross_key,
    cross_value,
    cross_out,
    feed_gain,
    gate_weight,
    up_weight,
    down_weight,
    upstream,
):
    tokens, seqs, width = inputs.shape
    mem_tokens = memory.shape[0]
    size = lax.axis_size("seq")
    length = tokens * size
    buckets = bias_table.shape[0]
    me = lax.axis_index("seq")

    def flat(array):
        return jnp.transpose(array, (1, 0, 2)).reshape(-1, array.shape[2])

    def unflat(array):
        return jnp.transpose(array.reshape(seqs, -1, array.shape[1]), (1, 0, 2))

    positions = me * tokens + jnp.arange(tokens, dtype=jnp.int32)
    live = (positions[None, :] < target_length[:, None]).reshape(-1, 1)
    held = me * mem_tokens + jnp.arange(mem_tokens, dtype=jnp.int32)
    held = (held[None, :] < memory_length[:, None]).reshape(-1, 1)
    me_line = me.astype(jnp.int32).reshape(1)
    self_info = jnp.concatenate([me_line, (me * tokens < target_length).astype(jnp.int32)])
    cross_info = jnp.concatenate([me_line, (memory_length + UNIT - 1) // UNIT])

    x = flat(inputs)
    xf = x.astype(f32)
    mem = jnp.where(held, flat(memory), 0)
    grad_low = jnp.where(live, flat(upstream), 0)
    rate_self = norm_rate(xf)
    normed_self = (xf * rate_self * self_gain).astype(bf16)
    keys = mm(normed_self, self_key).astype(bf16)
    values = mm(normed_self, self_value).astype(bf16)
    held_kv = gather_start(jnp.concatenate([keys, values], axis=1))
    memory_kv = jnp.concatenate(
        [mm(mem, cross_key).astype(bf16), mm(mem, cross_value).astype(bf16)], axis=1
    )
    gathered = gather_finish(held_kv)
    held_memory = gather_start(tie([memory_kv], held_kv[1:])[0])
    query = mm(normed_self, self_query).astype(bf16)
    bucket_match = distance_bucket[:, None] == jnp.arange(buckets, dtype=jnp.int32)[None, :]
    bucket_onehot = bucket_match.astype(f32)
    line = jnp.dot(bias_table.T, bucket_onehot.T, precision=highest, preferred_element_type=f32)
    line = jnp.concatenate([jnp.full((line.shape[0], 2 * tokens), negative, f32), line], axis=1)
    line = line.reshape(GROUPS // BATCH, -1, length + 2 * tokens)
    live_rows = live.astype(f32)
    low_own, low_other = core_halves(*cut(grad_low))
    low_pair = exchange(low_other, "seq", 1)
    mem_pair = exchange(mem, "seq", 1)

    self_mixed, self_logsum = attend(query, gathered, self_info, seqs, line)
    recalled = gather_finish(held_memory[:1] + tie(held_memory[1:], [self_mixed]))
    full, low_full, row = (x.shape, f32), (x.shape, bf16), ((1, width), f32)
    first, normed_cross, recall_query = whole_call(
        between_kernel,
        [full, low_full, (query.shape, bf16)],
        x,
        self_mixed,
        self_out,
        cross_gain.reshape(1, -1),
        cross_query,
        stream=True,
    )
    cross_mixed, cross_logsum = attend(recall_query, recalled, cross_info, seqs, None)
    core = (me % 2).astype(jnp.int32).reshape(1)
    normed_feed, hidden, gu_own, gu_other, outputs, second_grad, cross_mixed_grad, feed_gain_grad = feed_forward(
        core,
        first,
        cross_mixed,
        cross_out,
        live_rows,
        feed_gain,
        grad_low,
        gate_weight,
        up_weight,
        down_weight,
        [],
    )
    feed_pair = exchange(normed_feed, "seq", 1)
    hidden_pair = exchange(hidden, "seq", 1)
    gu_pair = exchange(gu_other, "seq", 1)
    hidden_cols = hidden.shape[1]
    tiles = hidden_cols // TILE
    cutting = tiles // 2
    gu_task = (((0, 0), (1, 0), (2, 0), (3, 0)), width)
    feed_chain = Chain.of(
        group_grads(
            [normed_feed, feed_pair, gu_own, gu_pair, hidden, hidden_pair, low_own, low_pair],
            [
                (((4, 0), (5, 0), (6, 0), (7, 0)), hidden_cols, [(0, 0), (1, TILE)]),
                gu_task + ([(0, j * TILE) for j in range(cutting)],),
                gu_task + ([(1, j * TILE) for j in range(cutting, tiles)],),
            ],
        )
    )
    before = [feed_chain.send[0]]
    feed_first = feed_chain.start()
    recall_query_grad, memory_kept, memory_rest = attend_back(
        recall_query, cross_mixed, cross_mixed_grad, cross_logsum, recalled, cross_info, seqs, None, before
    )
    first_grad, self_mixed_grad, grads_own, grads_other, cross_gain_grad = whole_call(
        between_back_kernel,
        [full, (query.shape, bf16), ((x.shape[0], 3 * width // 2), bf16), ((x.shape[0], 3 * width // 2), bf16), row],
        recall_query_grad,
        cross_query,
        second_grad,
        first,
        cross_gain.reshape(1, -1),
        self_out,
        core=core,
    )
    query_grad, kept, rest, line_grad = attend_back(
        query, self_mixed, self_mixed_grad, self_logsum, gathered, self_info, seqs, line
    )
    grads_pair = exchange(grads_other, "seq", 1)
    shared = jnp.concatenate(tie([normed_self, self_mixed, normed_cross, cross_mixed], before), axis=1)
    shared = exchange(shared, "seq", 1)

    memory_parts = scatter_start(memory_kept, memory_rest)
    kept, rest, query_grad = tie([kept, rest, query_grad], feed_first + [grads_pair, shared])
    key_parts = scatter_start(kept, rest)
    feed_chain.add()
    feed_second = feed_chain.start([kept])
    memory_sent = scatter_send(memory_parts[:1] + tie(memory_parts[1:], [kept]))
    query_own, query_other = core_halves(*cut(query_grad))
    query_pair = exchange(query_other, "seq", 1)
    two = [(0, 0), (1, TILE)]
    out_chain = Chain.of(
        group_grads(
            [cross_mixed, normed_cross, self_mixed, shared, grads_own, grads_pair],
            [
                (((0, 0), (3, 3 * width), (4, 0), (5, 0)), width, two),
                (((1, 0), (3, 2 * width), (4, width // 2), (5, width // 2)), width, two),
                (((2, 0), (3, width), (4, width), (5, width)), width, two),
            ],
            [query_grad],
        )
    )
    line_grad = line_grad.reshape(-1, line_grad.shape[2])[:, 2 * tokens :]
    table_grad = jnp.dot(line_grad, bucket_onehot, precision=highest, preferred_element_type=f32).T
    arrived = feed_second + key_parts[1:] + [query_pair, out_chain.send[0]]

    key_sent = scatter_send(key_parts[:1] + tie(key_parts[1:], arrived))
    out_first = out_chain.start(arrived)
    feed_chain.add()
    feed_chain.to_dp()
    feed_chain = Chain.merged([feed_chain])
    feed_z = feed_chain.start(arrived)
    key_half, key_half_pair = scatter_finish(key_parts[0], key_sent)
    memory_half, memory_half_pair = scatter_finish(memory_parts[0], memory_sent)
    arrived = key_sent + memory_sent

    in_chain = Chain.of(
        group_grads(
            [normed_self, shared, query_own, query_pair, key_half, key_half_pair, mem, mem_pair, memory_half, memory_half_pair],
            [
                (((6, 0), (7, 0), (8, 0), (9, 0)), width, two),
                (((0, 0), (1, 0), (2, 0), (3, 0)), width, two),
                (((0, 0), (1, 0), (4, 0), (5, 0)), width, two),
            ],
            arrived,
        )
    )
    in_first = in_chain.start()
    key_other, memory_other = [
        exchange(v, "seq", 1) for v in tie([key_half_pair, memory_half_pair], in_chain.send[:1])
    ]
    memory_key_low, memory_value_low = core_halves(memory_half, memory_other)
    memory_grad = mm_t(memory_key_low, cross_key) + mm_t(memory_value_low, cross_value)
    input_grad, self_gain_grad = whole_call(
        enter_back_kernel,
        [full, row],
        query_grad,
        key_half,
        key_other,
        self_query,
        self_key,
        self_value,
        x,
        self_gain.reshape(1, -1),
        first_grad,
        core=core,
        after=[in_chain.send[0]],
    )
    small = jnp.concatenate(
        [v.reshape(-1) for v in (self_gain_grad, cross_gain_grad, feed_gain_grad, table_grad)]
    ).reshape(-1, 128)
    small = sum_over(small, [("seq", 1)])
    out_chain.add()
    out_second = out_chain.start(arrived + in_chain.send[:1])
    feed_chain.add()
    feed_z = feed_chain.start(arrived)
    arrived = in_first + out_second + feed_z + [small]

    dp_bits, seq_bits = bits_of(lax.axis_size("dp"), 1), bits_of(lax.axis_size("seq"), 2)
    small = sum_over(tie([small], arrived)[0], [("dp", bit) for bit in dp_bits])
    in_chain.add()
    in_second = in_chain.start(arrived)
    out_chain.add()
    out_chain.to_dp()
    out_chain = Chain.merged([out_chain])
    out_z = out_chain.start(arrived)
    arrived = in_second + out_z

    in_chain.add()
    in_chain.to_dp()
    in_chain = Chain.merged([in_chain])
    in_z = in_chain.start(arrived)
    out_chain.add()
    out_z = out_chain.start(arrived)
    small = sum_over(tie([small], arrived)[0], [("seq", bit) for bit in seq_bits]).reshape(-1)

    blocks = 2 ** len(grad_order(False))
    narrow, broad = width // blocks, hidden_cols // blocks
    keep, got = feed_chain.last()
    gate_out, up_out, down_out = finish_rows(
        core,
        keep,
        got,
        [broad] + [narrow] * cutting + [broad] + [narrow] * (tiles - cutting),
        [
            ([1 + j for j in range(cutting)] + [2 + j for j in range(cutting, tiles)], False),
            ([0, 1 + cutting], True),
        ],
    )
    keep, got = out_chain.last()
    cross_out_out, cross_query_out, self_out_out = finish_rows(
        core, keep, got, [narrow] * 6, [([0, 3], True), ([1, 4], True), ([2, 5], True)]
    )
    keep, got = in_chain.last()
    cross_key_out, cross_value_out, self_query_out, self_key_out, self_value_out = finish_rows(
        core, keep, got, [narrow] * 6, [([0, 3], False), ([1, 4], True), ([2, 5], False)]
    )

    return (
        unflat(outputs),
        unflat(input_grad),
        unflat(memory_grad),
        small[:width],
        self_query_out,
        self_key_out,
        self_value_out,
        self_out_out,
        small[3 * width :].reshape(buckets, -1),
        small[width : 2 * width],
        cross_query_out,
        cross_key_out,
        cross_value_out,
        cross_out_out,
        small[2 * width : 3 * width],
        gate_out,
        up_out,
        down_out,
    )


def solution(mesh):
    placed = P("seq", "dp", None)
    rows = P(("dp", "seq"), None)
    return jax.shard_map(
        per_device,
        mesh=mesh,
        in_specs=(placed, placed, P("dp"), P("dp")) + (P(),) * 16 + (placed,),
        out_specs=(
            placed,
            placed,
            placed,
            P(),
            rows,
            rows,
            rows,
            rows,
            P(),
            P(),
            rows,
            rows,
            rows,
            rows,
            P(),
            rows,
            rows,
            rows,
        ),
        check_vma=False,
    )
```

```python
import functools

import jax
import jax.numpy as jnp
from jax import lax
from jax.experimental import pallas as pl
from jax.experimental.pallas import tpu as pltpu
from jax.sharding import PartitionSpec as P

GROUPS = 8


epsilon = 1e-06
scale = 0.125
negative = -1e30
highest = lax.Precision.HIGHEST
bf16 = jnp.bfloat16
f32 = jnp.float32


def norm_rate(value):
    return lax.rsqrt(jnp.mean(value * value, axis=-1, keepdims=True) + epsilon)


def norm_back(value, rate, gain, incoming):
    scaled = incoming * gain
    inner = jnp.mean(scaled * value, axis=-1, keepdims=True)
    grad = rate * (scaled - value * (rate * rate * inner))
    return grad, jnp.sum(incoming * value * rate, axis=0, keepdims=True)


def mm(left, right):
    return jnp.dot(left, right, preferred_element_type=f32)


def mm_t(grad, weight):
    return lax.dot_general(grad, weight, (((1,), (1,)), ((), ())), preferred_element_type=f32)


def exchange(value, axis, bit):
    size = lax.axis_size(axis)
    return lax.ppermute(value, axis, [(i, i ^ bit) for i in range(size)])


def bits_of(size, lowest):
    bits = []
    bit = lowest
    while bit < size:
        bits.append(bit)
        bit = bit * 2
    return bits


TILE = 256
LIGHT = pl.CostEstimate(flops=1, bytes_accessed=1, transcendentals=0)


def grad_order(flip):
    seq_bits = bits_of(lax.axis_size("seq"), 2)
    if flip:
        seq_bits = seq_bits[::-1]
    return [("seq", b) for b in seq_bits] + [("dp", b) for b in bits_of(lax.axis_size("dp"), 1)]


def grads_kernel(chips, orders, tasks, sources, count, me_ref, *refs):
    ins, refs = refs[:sources], refs[count:]
    outs, (turned, total) = refs[:4], refs[4:]
    blocks = 2 ** len(orders[0])
    filled = [0, 0]
    for (xo, xp, do, dp), tokens, rows, rchip, tiles in tasks:
        for half, (place, lane) in enumerate((xo, xp)):
            turned[:rows, half * tokens : (half + 1) * tokens] = ins[place][:, lane : lane + rows].T
        for stack, lane in tiles:
            value = mm(turned[:rows, :tokens], ins[do[0]][:, do[1] + lane : do[1] + lane + TILE])
            value = value + mm(
                turned[:rows, tokens : 2 * tokens], ins[dp[0]][:, dp[1] + lane : dp[1] + lane + TILE]
            )
            for block in range(blocks):
                total[block, :rchip] = value[block * rchip : (block + 1) * rchip]
            order = orders[stack]
            for slot in range(blocks):
                seq_part, dp_part = 0, 0
                for place, (axis, bit) in enumerate(order):
                    if (slot >> (len(order) - 1 - place)) & 1:
                        if axis == "seq":
                            seq_part = seq_part | (bit // 2)
                        else:
                            dp_part = dp_part | bit
                block = (me_ref[0] ^ dp_part) * chips + (me_ref[1] ^ seq_part)
                outs[2 * stack + slot // (blocks // 2)][
                    slot % (blocks // 2), filled[stack] : filled[stack] + rchip
                ] = total[block, :rchip].astype(bf16)
            filled[stack] += rchip


def block_whole(array):
    return pl.BlockSpec(array.shape, lambda i: (0,) * len(array.shape))


def group_grads(arrays, tasks, after=()):
    chips = lax.axis_size("seq") // 2
    orders = [grad_order(False), grad_order(True)]
    blocks = 2 ** len(orders[0])
    full = []
    depth = [0, 0]
    flops = 0
    for names, rows, tiles in tasks:
        tokens = arrays[names[0][0]].shape[0]
        full.append((names, tokens, rows, rows // blocks, tiles))
        flops += 4 * tokens * rows * TILE * len(tiles)
        for stack, lane in tiles:
            depth[stack] += rows // blocks
    me = jnp.stack([lax.axis_index("dp"), lax.axis_index("seq") // 2]).astype(jnp.int32)
    most = max(t[2] for t in full)
    shapes = [jax.ShapeDtypeStruct((blocks // 2, depth[i // 2], TILE), bf16) for i in range(4)]
    total = arrays[0].dtype.itemsize * sum(a.size for a in arrays)
    return pl.pallas_call(
        functools.partial(grads_kernel, chips, orders, full, len(arrays), len(arrays) + len(after)),
        grid=(1,),
        in_specs=[pl.BlockSpec(memory_space=pltpu.SMEM)]
        + [block_whole(a) for a in arrays]
        + [pl.BlockSpec(memory_space=pl.ANY)] * len(after),
        out_specs=[block_whole(a) for a in shapes],
        scratch_shapes=[
            pltpu.VMEM((most, max(2 * t[1] for t in full)), bf16),
            pltpu.VMEM((blocks, most // blocks, TILE), f32),
        ],
        out_shape=shapes,
        compiler_params=pltpu.CompilerParams(vmem_limit_bytes=60 * 1024 * 1024),
        cost_estimate=LIGHT,
    )(me, *arrays, *after)


class Chain:
    def __init__(self, keep, send, orders, level=0):
        self.keep, self.send, self.orders, self.level, self.got = keep, send, orders, level, None

    @staticmethod
    def of(outs):
        return Chain([outs[0], outs[2]], [outs[1], outs[3]], [grad_order(False), grad_order(True)])

    @staticmethod
    def merged(chains):
        level = chains[0].level
        if chains[0].orders[0][level][0] == "dp":
            keeps = [[k for c in chains for k in c.keep]]
            sends = [[v for c in chains for v in c.send]]
        else:
            keeps = [list(k) for k in zip(*[c.keep for c in chains])]
            sends = [list(v) for v in zip(*[c.send for c in chains])]
        joined = [[jnp.concatenate(v, axis=1) for v in group] for group in (keeps, sends)]
        return Chain(joined[0], joined[1], chains[0].orders[: len(keeps)], level)

    def start(self, tokens=()):
        if tokens:
            self.send = tie(self.send, tokens)
        self.got = [exchange(v, *self.orders[i][self.level]) for i, v in enumerate(self.send)]
        self.level += 1
        return self.got

    def add(self):
        got, self.got = self.got, None
        half = got[0].shape[0] // 2
        if half:
            self.send = [k[half:] + g[half:] for k, g in zip(self.keep, got)]
            self.keep = [k[:half] + g[:half] for k, g in zip(self.keep, got)]
        else:
            self.keep = [k.astype(f32) + g.astype(f32) for k, g in zip(self.keep, got)]

    def to_dp(self):
        while self.orders[0][self.level][0] == "seq":
            self.start()
            self.add()

    def last(self):
        while self.level < len(self.orders[0]):
            if self.got is not None:
                self.add()
            self.start()
        return self.keep[0], self.got[0]


def split_kernel(tiles, core_ref, keep, got, mine, other):
    first = core_ref[0] == 0
    start = 0
    for row, rows in tiles:
        half = rows // 2
        value = keep[0, row : row + rows].astype(f32) + got[0, row : row + rows].astype(f32)
        low, high = value[:half], value[half:]
        mine[start : start + half] = jnp.where(first, low, high)
        other[start : start + half] = jnp.where(first, high, low).astype(bf16)
        start += half


def place_kernel(weights, core_ref, mine, got, *outs):
    first = core_ref[0] == 0
    for tiles, half, (left, shift_left), (right, shift_right) in weights:
        for i, row in enumerate(tiles):
            own, swapped = mine[row : row + half], got[row : row + half].astype(f32)
            outs[left][:, shift_left + i * TILE : shift_left + (i + 1) * TILE] = jnp.where(first, own, swapped)
            outs[right][:, shift_right + i * TILE : shift_right + (i + 1) * TILE] = jnp.where(first, swapped, own)


def finish_rows(core, keep, got, tiles, weights, after=()):
    starts, total = [], 0
    listed = []
    for rows in tiles:
        listed.append((2 * total, rows))
        starts.append(total)
        total += rows // 2
    mine, other = whole_call(
        functools.partial(split_kernel, listed), [((total, TILE), f32), ((total, TILE), bf16)], keep, got, core=core, after=after
    )
    arrived = exchange(other, "seq", 1)
    shapes, plan = [], []
    for places, joined in weights:
        half, columns = tiles[places[0]] // 2, len(places) * TILE
        rows = [starts[p] for p in places]
        if joined:
            plan.append((rows, half, (len(shapes), 0), (len(shapes), columns)))
            shapes.append(((half, 2 * columns), f32))
        else:
            plan.append((rows, half, (len(shapes), 0), (len(shapes) + 1, 0)))
            shapes += [((half, columns), f32)] * 2
    return whole_call(functools.partial(place_kernel, plan), shapes, mine, arrived, core=core)


def core_halves(left, right):
    core = lax.axis_index("seq") % 2
    return jnp.where(core == 0, left, right), jnp.where(core == 0, right, left)


def pair_grad(left, right):
    mine, other = core_halves(left, right)
    return mine, exchange(other, "seq", 1)


def cut(value):
    half = value.shape[1] // 2
    return value[:, :half], value[:, half:]


def tie(values, tokens):
    done = lax.optimization_barrier((tuple(values), tuple(tokens)))
    return list(done[0])


def gather_start(value):
    chips = lax.axis_size("seq") // 2
    return [value] + [exchange(value, "seq", 2 * chip) for chip in range(1, chips)]


def gather_finish(mine):
    own = exchange(mine[0], "seq", 1)
    rest = exchange(jnp.concatenate(mine[1:], axis=1), "seq", 1)
    pieces = []
    for chip, value in enumerate(mine):
        pieces.append((value, 0))
        pieces.append((own, 0) if chip == 0 else (rest, chip - 1))
    return pieces


def scatter_start(mine, other):
    got = exchange(other, "seq", 1)
    parts = []
    for chip in range(mine.shape[0] // 2):
        pair = slice(2 * chip, 2 * chip + 2)
        part = mine[pair].astype(f32) + got[pair].astype(f32)
        parts.append(part if chip == 0 else part.astype(bf16))
    return parts


def scatter_send(parts):
    return [exchange(part, "seq", 2 * (chip + 1)) for chip, part in enumerate(parts[1:])]


def scatter_finish(part, arrived):
    total = part
    for value in arrived:
        total = total + value.astype(f32)
    total = total.astype(bf16)
    return total[0], total[1]


def sum_over(value, steps):
    for axis, bit in steps:
        value = value + exchange(value, axis, bit)
    return value


UNIT = 256


def nt(left, right):
    return lax.dot_general(left, right, (((1,), (1,)), ((), ())), preferred_element_type=f32)


def make_strip(e_ref, strip, tokens):
    heads, parts = strip.shape[0], strip.shape[1]
    for h in range(heads):
        line = e_ref[0, h : h + 1, :]
        turned = pltpu.roll(
            jnp.broadcast_to(line, (tokens, line.shape[1])), 0, 1, stride=1, stride_axis=0
        )
        for d in range(parts):
            strip[h, d] = turned[:, tokens * (d + 1) : tokens * (d + 2)]


def two_heads(ref, rows, lane, head):
    return jnp.concatenate(
        [ref[rows, lane : lane + head], ref[rows, lane + head : lane + 2 * head]], axis=0
    )


def unit_rows(refs, unit, per_unit, count, s, lane, head):
    return jnp.concatenate(
        [
            refs[unit * per_unit + p][s * count : (s + 1) * count, lane : lane + head]
            for p in range(per_unit)
        ],
        axis=0,
    )


def unit_bias(strip, me, unit, per_unit, group):
    rows = []
    for p in range(per_unit):
        place = me - (me ^ (unit * per_unit + p)) + 1
        rows.append(jnp.concatenate([strip[2 * group, place], strip[2 * group + 1, place]], axis=1))
    return jnp.concatenate(rows, axis=0)


def attend_kernel(biased, seqs, tokens, count, pieces, batch, *refs):
    info, refs = refs[0], refs[1:]
    if biased:
        e_ref, refs = refs[0], refs[1:]
    q_ref, refs = refs[0], refs[1:]
    k_refs, v_refs = refs[:pieces], refs[pieces : 2 * pieces]
    out_ref, lse_ref, peak, total, mixed, queries = refs[2 * pieces : 2 * pieces + 6]
    if biased:
        strip = refs[2 * pieces + 6]
        make_strip(e_ref, strip, tokens)
    per_unit = UNIT // count
    units = pieces // per_unit
    me = info[0]
    mine = me // per_unit
    head = q_ref.shape[1] // (2 * batch)
    for s in range(seqs):
        rows = slice(s * tokens, (s + 1) * tokens)

        @pl.when(info[1 + s] > 0)
        def _(s=s, rows=rows):
            for g in range(batch):
                queries[g] = two_heads(q_ref, rows, 2 * g * head, head) * scale
            peak[...] = jnp.full(peak.shape, -3e38, f32)
            total[...] = jnp.zeros(total.shape, f32)
            mixed[...] = jnp.zeros(mixed.shape, f32)
            for unit in range(units):
                if biased:
                    used = (unit ^ mine) <= mine
                else:
                    used = (unit ^ mine) < info[1 + s]

                @pl.when(used)
                def _(unit=unit):
                    states = []
                    for g in range(batch):
                        k = unit_rows(k_refs, unit, per_unit, count, s, g * head, head)
                        scores = nt(k, queries[g])
                        if biased:
                            scores = scores + unit_bias(strip, me, unit, per_unit, g)
                        states.append((scores, peak[g], total[g], mixed[g]))
                    done = []
                    for g, (scores, old, summed, part) in enumerate(states):
                        v = unit_rows(v_refs, unit, per_unit, count, s, g * head, head)
                        top = jnp.maximum(old, jnp.max(scores, axis=0, keepdims=True))
                        raised = jnp.exp(scores - top)
                        fade = jnp.exp(old - top)
                        done.append(
                            (
                                top,
                                summed * fade + jnp.sum(raised, axis=0, keepdims=True),
                                part * fade + mm(v.T, raised.astype(bf16)),
                            )
                        )
                    for g in range(batch):
                        peak[g], total[g], mixed[g] = done[g]

            for g in range(batch):
                lse_ref[0, batch * s + g : batch * s + g + 1, :] = peak[g] + jnp.log(total[g])
                done = (mixed[g] / total[g]).T.astype(bf16)
                out_ref[rows, 2 * g * head : 2 * (g + 1) * head] = jnp.concatenate(
                    [done[:tokens], done[tokens:]], axis=1
                )

        @pl.when(info[1 + s] <= 0)
        def _(s=s, rows=rows):
            lse_ref[0, batch * s : batch * (s + 1), :] = jnp.zeros((batch, 2 * tokens), f32)
            out_ref[rows, :] = jnp.zeros((tokens, out_ref.shape[1]), bf16)


def back_kernel(biased, seqs, tokens, count, pieces, after, batch, *refs):
    info, refs = refs[0], refs[1 + after :]
    if biased:
        e_ref, refs = refs[0], refs[1:]
    q_ref, o_ref, do_ref, lse_ref, refs = refs[0], refs[1], refs[2], refs[3], refs[4:]
    k_refs, v_refs, refs = refs[:pieces], refs[pieces : 2 * pieces], refs[2 * pieces :]
    dq_ref, keep, send, refs = refs[0], refs[1], refs[2], refs[3:]
    if biased:
        table_ref, refs = refs[0], refs[1:]
    dq, queries, grads, inner = refs[:4]
    if biased:
        strip, sums = refs[4:]
        make_strip(e_ref, strip, tokens)
        sums[...] = jnp.zeros(sums.shape, f32)
    per_unit = UNIT // count
    units = pieces // per_unit
    me = info[0]
    mine = me // per_unit
    first = me % 2 == 0
    head = q_ref.shape[1] // (2 * batch)
    for s in range(seqs):
        rows = slice(s * tokens, (s + 1) * tokens)
        keys = slice(s * count, (s + 1) * count)

        def clear(unit, keys=keys):
            for p in range(per_unit):
                piece = unit * per_unit + p
                keep[piece, keys, :] = jnp.zeros((count, batch * head), bf16)
                send[piece ^ 1, keys, :] = jnp.zeros((count, batch * head), bf16)

        @pl.when(info[1 + s] > 0)
        def _(s=s, rows=rows, keys=keys, clear=clear):
            for g in range(batch):
                lane = 2 * g * head
                queries[g] = two_heads(q_ref, rows, lane, head) * scale
                do2 = two_heads(do_ref, rows, lane, head)
                o2 = two_heads(o_ref, rows, lane, head)
                grads[g] = do2
                inner[g] = jnp.sum((o2.astype(f32) * do2.astype(f32)).T, axis=0, keepdims=True)
            dq[...] = jnp.zeros(dq.shape, f32)
            for unit in range(units):
                if biased:
                    used = (unit ^ mine) <= mine
                else:
                    used = (unit ^ mine) < info[1 + s]

                @pl.when(used)
                def _(unit=unit):
                    states = []
                    for g in range(batch):
                        k = unit_rows(k_refs, unit, per_unit, count, s, g * head, head)
                        v = unit_rows(v_refs, unit, per_unit, count, s, g * head, head)
                        scores = nt(k, queries[g])
                        if biased:
                            scores = scores + unit_bias(strip, me, unit, per_unit, g)
                        states.append((k, scores, nt(v, grads[g])))
                    done, turned = [], []
                    for g, (k, scores, down) in enumerate(states):
                        share = jnp.exp(scores - lse_ref[0, batch * s + g : batch * s + g + 1, :])
                        grad = (share * (down - inner[g])).astype(bf16)
                        dv = mm(share.astype(bf16), grads[g])
                        dk = mm(grad, queries[g])
                        turned.append(mm(k.T, grad))
                        done.append(
                            (
                                grad,
                                jnp.where(first, dk, dv).astype(bf16),
                                jnp.where(first, dv, dk).astype(bf16),
                            )
                        )
                    for g in range(batch):
                        dq[g] += turned[g]
                    kept = jnp.concatenate([d[1] for d in done], axis=1)
                    sent = jnp.concatenate([d[2] for d in done], axis=1)
                    for p in range(per_unit):
                        piece = unit * per_unit + p
                        part = slice(p * count, (p + 1) * count)
                        keep[piece, keys, :] = kept[part]
                        send[piece ^ 1, keys, :] = sent[part]
                        if biased:
                            place = me - (me ^ piece) + 1
                            for g in range(batch):
                                for h in range(2):
                                    sums[2 * g + h, place] += done[g][0][
                                        part, h * tokens : (h + 1) * tokens
                                    ].astype(f32)

                @pl.when(jnp.logical_not(used))
                def _(unit=unit):
                    clear(unit)

            for g in range(batch):
                done = (dq[g] * scale).T.astype(bf16)
                dq_ref[rows, 2 * g * head : 2 * (g + 1) * head] = jnp.concatenate(
                    [done[:tokens], done[tokens:]], axis=1
                )

        @pl.when(info[1 + s] <= 0)
        def _(rows=rows, clear=clear):
            for unit in range(units):
                clear(unit)
            dq_ref[rows, :] = jnp.zeros((tokens, dq_ref.shape[1]), bf16)

    if biased:
        parts = sums.shape[1]
        span = tokens * (parts + 1)
        for h in range(2 * batch):
            line = jnp.concatenate(
                [jnp.zeros((tokens, tokens), f32)] + [sums[h, d] for d in range(parts)], axis=1
            )
            height = tokens
            while height > 8:
                height = height // 2
                line = line[:height] + pltpu.roll(line[height:], span - height, 1)
            while height > 1:
                height = height // 2
                upper = pltpu.roll(line, span - height, 1)
                line = line[:height] + upper[height : 2 * height]
            table_ref[0, h : h + 1, :] = line


def block_of(array, lanes, offset=0):
    return pl.BlockSpec((array.shape[0], lanes), lambda i, info: (0, offset + i))


BATCH = 4


def attend(query, pieces, info, seqs, line):
    tokens = query.shape[0] // seqs
    arrays = [p[0] for p in pieces]
    count = arrays[0].shape[0] // seqs
    n = len(pieces)
    steps = GROUPS // BATCH
    wide, narrow = query.shape[1] // steps, arrays[0].shape[1] // 2 // steps
    places = [2 * steps * p[1] for p in pieces]
    head = narrow // BATCH
    biased = line is not None
    scratch = [pltpu.VMEM((BATCH, 1, 2 * tokens), f32)] * 2 + [
        pltpu.VMEM((BATCH, head, 2 * tokens), f32),
        pltpu.VMEM((BATCH, 2 * tokens, head), bf16),
    ]
    extra = []
    if biased:
        scratch.append(pltpu.VMEM((2 * BATCH, n + 1, tokens, tokens), f32))
        extra = [pl.BlockSpec((1, 2 * BATCH, line.shape[2]), lambda i, info: (i, 0, 0))]
    pairs = n * count * seqs * tokens * GROUPS * 2
    return pl.pallas_call(
        functools.partial(attend_kernel, biased, seqs, tokens, count, n, BATCH),
        grid_spec=pltpu.PrefetchScalarGridSpec(
            num_scalar_prefetch=1,
            grid=(steps,),
            in_specs=extra
            + [block_of(query, wide)]
            + [block_of(a, narrow, p) for a, p in zip(arrays, places)]
            + [block_of(a, narrow, p + steps) for a, p in zip(arrays, places)],
            out_specs=[
                block_of(query, wide),
                pl.BlockSpec((1, BATCH * seqs, 2 * tokens), lambda i, info: (i, 0, 0)),
            ],
            scratch_shapes=scratch,
        ),
        out_shape=[
            jax.ShapeDtypeStruct(query.shape, bf16),
            jax.ShapeDtypeStruct((steps, BATCH * seqs, 2 * tokens), f32),
        ],
        compiler_params=pltpu.CompilerParams(vmem_limit_bytes=40 * 1024 * 1024),
        cost_estimate=pl.CostEstimate(flops=4096 * pairs, bytes_accessed=8 * query.size, transcendentals=pairs),
    )(info, *([line] if biased else []), query, *arrays, *arrays)


def attend_back(query, mixed, upstream, logsum, pieces, info, seqs, line, after=()):
    tokens = query.shape[0] // seqs
    arrays = [p[0] for p in pieces]
    count = arrays[0].shape[0] // seqs
    n = len(pieces)
    steps = GROUPS // BATCH
    wide, narrow = query.shape[1] // steps, arrays[0].shape[1] // 2 // steps
    places = [2 * steps * p[1] for p in pieces]
    head = narrow // BATCH
    biased = line is not None
    scratch = [
        pltpu.VMEM((BATCH, head, 2 * tokens), f32),
        pltpu.VMEM((BATCH, 2 * tokens, head), bf16),
        pltpu.VMEM((BATCH, 2 * tokens, head), bf16),
        pltpu.VMEM((BATCH, 1, 2 * tokens), f32),
    ]
    extra, extra_out, extra_shape = [], [], []
    if biased:
        scratch += [pltpu.VMEM((2 * BATCH, n + 1, tokens, tokens), f32)] * 2
        extra = [pl.BlockSpec((1, 2 * BATCH, line.shape[2]), lambda i, info: (i, 0, 0))]
        extra_out = [pl.BlockSpec((1, 2 * BATCH, tokens * (n + 2)), lambda i, info: (i, 0, 0))]
        extra_shape = [jax.ShapeDtypeStruct((steps, 2 * BATCH, tokens * (n + 2)), f32)]
    part = pl.BlockSpec((n, seqs * count, narrow), lambda i, info: (0, 0, i))
    part_shape = jax.ShapeDtypeStruct((n, seqs * count, narrow * steps), bf16)
    pairs = n * count * seqs * tokens * GROUPS * 2
    return pl.pallas_call(
        functools.partial(back_kernel, biased, seqs, tokens, count, n, len(after), BATCH),
        grid_spec=pltpu.PrefetchScalarGridSpec(
            num_scalar_prefetch=1,
            grid=(steps,),
            in_specs=[pl.BlockSpec(memory_space=pl.ANY)] * len(after)
            + extra
            + [block_of(query, wide)] * 3
            + [pl.BlockSpec((1, BATCH * seqs, 2 * tokens), lambda i, info: (i, 0, 0))]
            + [block_of(a, narrow, p) for a, p in zip(arrays, places)]
            + [block_of(a, narrow, p + steps) for a, p in zip(arrays, places)],
            out_specs=[block_of(query, wide), part, part] + extra_out,
            scratch_shapes=scratch,
        ),
        out_shape=[jax.ShapeDtypeStruct(query.shape, bf16), part_shape, part_shape] + extra_shape,
        compiler_params=pltpu.CompilerParams(vmem_limit_bytes=44 * 1024 * 1024),
        cost_estimate=LIGHT,
    )(info, *after, *([line] if biased else []), query, mixed, upstream, logsum, *arrays, *arrays)


def feed_kernel(core_ref, first_ref, mixed, out_w, live, gain, grad_low, gate_w, up_w, down_w, normed, hidden, own, pair, outputs, grad, mixed_grad, gain_grad, second, result, feed_in):
    step = pl.program_id(0)

    @pl.when(step == 0)
    def _():
        value = first_ref[...] + mm(mixed[...], out_w[...])
        second[...] = value
        normed[...] = (value * norm_rate(value) * gain[...]).astype(bf16)
        result[...] = jnp.zeros(result.shape, f32)
        feed_in[...] = jnp.zeros(feed_in.shape, f32)

    gate = mm(normed[...], gate_w[...])
    upper = mm(normed[...], up_w[...])
    incoming = nt(grad_low[...], down_w[...])
    square = gate * gate
    slope = 0.7978845608028654 * 0.044715
    bend = jnp.tanh(gate * (0.7978845608028654 + slope * square))
    rise = 0.5 * (1.0 + bend)
    curve = gate * rise
    steep = rise + 0.5 * gate * (1.0 - bend * bend) * (0.7978845608028654 + 3.0 * slope * square)
    acted = (curve * upper).astype(bf16)
    gate_grad = (incoming * upper * steep).astype(bf16)
    upper_grad = (incoming * curve).astype(bf16)
    hidden[...] = acted
    first = core_ref[0] == 0
    own[...] = jnp.where(first, gate_grad, upper_grad)
    pair[...] = jnp.where(first, upper_grad, gate_grad)
    result[...] += mm(acted, down_w[...])
    feed_in[...] += nt(gate_grad, gate_w[...]) + nt(upper_grad, up_w[...])

    @pl.when(step == pl.num_programs(0) - 1)
    def _():
        value = second[...]
        outputs[...] = ((value + result[...]) * live[...]).astype(bf16)
        part, gained = norm_back(value, norm_rate(value), gain[...], feed_in[...])
        total = grad_low[...].astype(f32) + part
        grad[...] = total
        gain_grad[...] = gained
        mixed_grad[...] = nt(total.astype(bf16), out_w[...]).astype(bf16)


def feed_forward(core, first, mixed, out_weight, live, gain, grad_low, gate_weight, up_weight, down_weight, after):
    tokens, width = first.shape
    units = gate_weight.shape[1]
    whole = pl.BlockSpec((tokens, width), lambda i: (0, 0))
    line = pl.BlockSpec((1, width), lambda i: (0, 0))
    tall = pl.BlockSpec((width, TILE), lambda i: (0, i))
    part = pl.BlockSpec((tokens, TILE), lambda i: (0, i))
    part_shape = jax.ShapeDtypeStruct((tokens, units), bf16)
    low_shape = jax.ShapeDtypeStruct((tokens, width), bf16)
    skip = len(after)

    def body(core_ref, *refs):
        feed_kernel(core_ref, *refs[skip:])

    return pl.pallas_call(
        body,
        grid=(units // TILE,),
        in_specs=[pl.BlockSpec(memory_space=pltpu.SMEM)]
        + [pl.BlockSpec(memory_space=pl.ANY)] * skip
        + [
            whole,
            whole,
            pl.BlockSpec(out_weight.shape, lambda i: (0, 0)),
            pl.BlockSpec((tokens, 1), lambda i: (0, 0)),
            line,
            whole,
            tall,
            tall,
            pl.BlockSpec((TILE, width), lambda i: (i, 0)),
        ],
        out_specs=[whole, part, part, part, whole, whole, whole, line],
        out_shape=[low_shape]
        + [part_shape] * 3
        + [
            low_shape,
            jax.ShapeDtypeStruct((tokens, width), f32),
            low_shape,
            jax.ShapeDtypeStruct((1, width), f32),
        ],
        scratch_shapes=[pltpu.VMEM((tokens, width), f32)] * 3,
        compiler_params=pltpu.CompilerParams(vmem_limit_bytes=60 * 1024 * 1024),
        cost_estimate=pl.CostEstimate(
            flops=12 * tokens * width * units, bytes_accessed=6 * width * units, transcendentals=tokens * units
        ),
    )(core, *after, first, mixed, out_weight, live, gain.reshape(1, -1), grad_low, gate_weight, up_weight, down_weight)


def between_kernel(x, mixed, out_w, gain, query_w, first, normed, query):
    value = x[...].astype(f32) + mm(mixed[...], out_w[...])
    first[...] = value
    low = (value * norm_rate(value) * gain[...]).astype(bf16)
    normed[...] = low
    query[...] = mm(low, query_w[...]).astype(bf16)


def between_back_kernel(core_ref, query_grad, query_w, second_grad, first_ref, gain, out_w, grad, mixed_grad, own, other, gain_grad):
    value = first_ref[...]
    part, gained = norm_back(value, norm_rate(value), gain[...], nt(query_grad[...], query_w[...]))
    total = second_grad[...] + part
    grad[...] = total
    gain_grad[...] = gained
    low = total.astype(bf16)
    mixed_grad[...] = nt(low, out_w[...]).astype(bf16)
    first = core_ref[0] == 0
    half = low.shape[1] // 2
    for i, array in enumerate((second_grad[...].astype(bf16), query_grad[...], low)):
        left, right = array[:, :half], array[:, half:]
        own[:, i * half : (i + 1) * half] = jnp.where(first, left, right)
        other[:, i * half : (i + 1) * half] = jnp.where(first, right, left)


def enter_back_kernel(core_ref, query_grad, half, rest, query_w, key_w, value_w, x, gain, first_grad, grad, gain_grad):
    first = core_ref[0] == 0
    keys = jnp.where(first, half[...], rest[...])
    values = jnp.where(first, rest[...], half[...])
    incoming = nt(query_grad[...], query_w[...]) + nt(keys, key_w[...]) + nt(values, value_w[...])
    value = x[...].astype(f32)
    part, gained = norm_back(value, norm_rate(value), gain[...], incoming)
    grad[...] = first_grad[...] + part
    gain_grad[...] = gained


def whole_call(kernel, shapes, *arrays, core=None, after=(), stream=False):
    vmem = pl.BlockSpec(memory_space=pltpu.VMEM)
    scalars = [] if core is None else [core]
    skip, lead = len(after), len(scalars)

    def body(*refs):
        kernel(*refs[:lead], *refs[lead + skip :])

    grid, spec, limit = {}, lambda array: vmem, 32
    if stream:
        grid, spec, limit = {"grid": (1,)}, block_whole, 60
    outs = [jax.ShapeDtypeStruct(*shape) for shape in shapes]
    return pl.pallas_call(
        body,
        **grid,
        in_specs=[pl.BlockSpec(memory_space=pltpu.SMEM)] * lead
        + [pl.BlockSpec(memory_space=pl.ANY)] * skip
        + [spec(a) for a in arrays],
        out_specs=[spec(a) for a in outs],
        out_shape=outs,
        compiler_params=pltpu.CompilerParams(vmem_limit_bytes=limit * 1024 * 1024),
        cost_estimate=LIGHT,
    )(*scalars, *after, *arrays)


def per_device(
    inputs,
    memory,
    target_length,
    memory_length,
    distance_bucket,
    bias_table,
    self_gain,
    self_query,
    self_key,
    self_value,
    self_out,
    cross_gain,
    cross_query,
    cross_key,
    cross_value,
    cross_out,
    feed_gain,
    gate_weight,
    up_weight,
    down_weight,
    upstream,
):
    tokens, seqs, width = inputs.shape
    mem_tokens = memory.shape[0]
    size = lax.axis_size("seq")
    length = tokens * size
    buckets = bias_table.shape[0]
    me = lax.axis_index("seq")

    def flat(array):
        return jnp.transpose(array, (1, 0, 2)).reshape(-1, array.shape[2])

    def unflat(array):
        return jnp.transpose(array.reshape(seqs, -1, array.shape[1]), (1, 0, 2))

    positions = me * tokens + jnp.arange(tokens, dtype=jnp.int32)
    live = (positions[None, :] < target_length[:, None]).reshape(-1, 1)
    held = me * mem_tokens + jnp.arange(mem_tokens, dtype=jnp.int32)
    held = (held[None, :] < memory_length[:, None]).reshape(-1, 1)
    me_line = me.astype(jnp.int32).reshape(1)
    self_info = jnp.concatenate([me_line, (me * tokens < target_length).astype(jnp.int32)])
    cross_info = jnp.concatenate([me_line, (memory_length + UNIT - 1) // UNIT])

    x = flat(inputs)
    xf = x.astype(f32)
    mem = jnp.where(held, flat(memory), 0)
    grad_low = jnp.where(live, flat(upstream), 0)
    rate_self = norm_rate(xf)
    normed_self = (xf * rate_self * self_gain).astype(bf16)
    keys = mm(normed_self, self_key).astype(bf16)
    values = mm(normed_self, self_value).astype(bf16)
    held_kv = gather_start(jnp.concatenate([keys, values], axis=1))
    memory_kv = jnp.concatenate(
        [mm(mem, cross_key).astype(bf16), mm(mem, cross_value).astype(bf16)], axis=1
    )
    gathered = gather_finish(held_kv)
    held_memory = gather_start(tie([memory_kv], held_kv[1:])[0])
    query = mm(normed_self, self_query).astype(bf16)
    bucket_match = distance_bucket[:, None] == jnp.arange(buckets, dtype=jnp.int32)[None, :]
    bucket_onehot = bucket_match.astype(f32)
    line = jnp.dot(bias_table.T, bucket_onehot.T, precision=highest, preferred_element_type=f32)
    line = jnp.concatenate([jnp.full((line.shape[0], 2 * tokens), negative, f32), line], axis=1)
    line = line.reshape(GROUPS // BATCH, -1, length + 2 * tokens)
    live_rows = live.astype(f32)
    low_own, low_other = core_halves(*cut(grad_low))
    low_pair = exchange(low_other, "seq", 1)
    mem_pair = exchange(mem, "seq", 1)

    self_mixed, self_logsum = attend(query, gathered, self_info, seqs, line)
    recalled = gather_finish(held_memory[:1] + tie(held_memory[1:], [self_mixed]))
    full, low_full, row = (x.shape, f32), (x.shape, bf16), ((1, width), f32)
    first, normed_cross, recall_query = whole_call(
        between_kernel,
        [full, low_full, (query.shape, bf16)],
        x,
        self_mixed,
        self_out,
        cross_gain.reshape(1, -1),
        cross_query,
        stream=True,
    )
    cross_mixed, cross_logsum = attend(recall_query, recalled, cross_info, seqs, None)
    core = (me % 2).astype(jnp.int32).reshape(1)
    normed_feed, hidden, gu_own, gu_other, outputs, second_grad, cross_mixed_grad, feed_gain_grad = feed_forward(
        core,
        first,
        cross_mixed,
        cross_out,
        live_rows,
        feed_gain,
        grad_low,
        gate_weight,
        up_weight,
        down_weight,
        [low_pair],
    )
    feed_pair = exchange(normed_feed, "seq", 1)
    hidden_pair = exchange(hidden, "seq", 1)
    gu_pair = exchange(gu_other, "seq", 1)
    hidden_cols = hidden.shape[1]
    tiles = hidden_cols // TILE
    cutting = tiles // 2
    gu_task = (((0, 0), (1, 0), (2, 0), (3, 0)), width)
    feed_chain = Chain.of(
        group_grads(
            [normed_feed, feed_pair, gu_own, gu_pair, hidden, hidden_pair, low_own, low_pair],
            [
                (((4, 0), (5, 0), (6, 0), (7, 0)), hidden_cols, [(0, 0), (1, TILE)]),
                gu_task + ([(0, j * TILE) for j in range(cutting)],),
                gu_task + ([(1, j * TILE) for j in range(cutting, tiles)],),
            ],
        )
    )
    before = [feed_chain.send[0]]
    feed_first = feed_chain.start()
    recall_query_grad, memory_kept, memory_rest = attend_back(
        recall_query, cross_mixed, cross_mixed_grad, cross_logsum, recalled, cross_info, seqs, None, before
    )
    first_grad, self_mixed_grad, grads_own, grads_other, cross_gain_grad = whole_call(
        between_back_kernel,
        [full, (query.shape, bf16), ((x.shape[0], 3 * width // 2), bf16), ((x.shape[0], 3 * width // 2), bf16), row],
        recall_query_grad,
        cross_query,
        second_grad,
        first,
        cross_gain.reshape(1, -1),
        self_out,
        core=core,
    )
    query_grad, kept, rest, line_grad = attend_back(
        query, self_mixed, self_mixed_grad, self_logsum, gathered, self_info, seqs, line
    )
    grads_pair = exchange(grads_other, "seq", 1)
    shared = jnp.concatenate(tie([normed_self, self_mixed, normed_cross, cross_mixed], before), axis=1)
    shared = exchange(shared, "seq", 1)

    memory_parts = scatter_start(memory_kept, memory_rest)
    kept, rest, query_grad = tie([kept, rest, query_grad], feed_first + [grads_pair, shared])
    key_parts = scatter_start(kept, rest)
    feed_chain.add()
    feed_second = feed_chain.start([kept])
    query_own, query_other = core_halves(*cut(query_grad))
    query_pair = exchange(query_other, "seq", 1)
    two = [(0, 0), (1, TILE)]
    out_chain = Chain.of(
        group_grads(
            [cross_mixed, normed_cross, self_mixed, shared, grads_own, grads_pair],
            [
                (((0, 0), (3, 3 * width), (4, 0), (5, 0)), width, two),
                (((1, 0), (3, 2 * width), (4, width // 2), (5, width // 2)), width, two),
                (((2, 0), (3, width), (4, width), (5, width)), width, two),
            ],
            [query_grad],
        )
    )
    line_grad = line_grad.reshape(-1, line_grad.shape[2])[:, 2 * tokens :]
    table_grad = jnp.dot(line_grad, bucket_onehot, precision=highest, preferred_element_type=f32).T
    arrived = feed_second + key_parts[1:] + memory_parts[1:] + [query_pair, out_chain.send[0]]

    joint = [jnp.concatenate(pair, axis=1) for pair in zip(key_parts[1:], memory_parts[1:])]
    joint_sent = scatter_send(key_parts[:1] + tie(joint, arrived))
    cut_at = key_parts[0].shape[1]
    key_sent = [v[:, :cut_at] for v in joint_sent]
    memory_sent = [v[:, cut_at:] for v in joint_sent]
    out_first = out_chain.start(arrived)
    feed_chain.add()
    feed_chain.to_dp()
    feed_chain = Chain.merged([feed_chain])
    feed_z = feed_chain.start(arrived)
    key_half, key_half_pair = scatter_finish(key_parts[0], key_sent)
    memory_half, memory_half_pair = scatter_finish(memory_parts[0], memory_sent)
    arrived = joint_sent + feed_z
    feed_chain.add()
    feed_z = feed_chain.start(arrived)

    in_chain = Chain.of(
        group_grads(
            [normed_self, shared, query_own, query_pair, key_half, key_half_pair, mem, mem_pair, memory_half, memory_half_pair],
            [
                (((6, 0), (7, 0), (8, 0), (9, 0)), width, two),
                (((0, 0), (1, 0), (2, 0), (3, 0)), width, two),
                (((0, 0), (1, 0), (4, 0), (5, 0)), width, two),
            ],
            arrived,
        )
    )
    in_first = in_chain.start()
    key_other, memory_other = [
        exchange(v, "seq", 1) for v in tie([key_half_pair, memory_half_pair], in_chain.send[:1])
    ]
    memory_key_low, memory_value_low = core_halves(memory_half, memory_other)
    memory_grad = mm_t(memory_key_low, cross_key) + mm_t(memory_value_low, cross_value)
    input_grad, self_gain_grad = whole_call(
        enter_back_kernel,
        [full, row],
        query_grad,
        key_half,
        key_other,
        self_query,
        self_key,
        self_value,
        x,
        self_gain.reshape(1, -1),
        first_grad,
        core=core,
        after=[in_chain.send[0]] + feed_z,
    )
    small = jnp.concatenate(
        [v.reshape(-1) for v in (self_gain_grad, cross_gain_grad, feed_gain_grad, table_grad)]
    ).reshape(-1, 128)
    small = sum_over(small, [("seq", 1)])
    out_chain.add()
    out_second = out_chain.start(arrived + in_chain.send[:1])
    arrived = in_first + out_second + [small]

    dp_bits, seq_bits = bits_of(lax.axis_size("dp"), 1), bits_of(lax.axis_size("seq"), 2)
    small = sum_over(tie([small], arrived)[0], [("dp", bit) for bit in dp_bits])
    in_chain.add()
    in_second = in_chain.start(arrived)
    out_chain.add()
    out_chain.to_dp()
    out_chain = Chain.merged([out_chain])
    out_z = out_chain.start(arrived)
    arrived = in_second + out_z

    in_chain.add()
    in_chain.to_dp()
    in_chain = Chain.merged([in_chain])
    in_z = in_chain.start(arrived)
    out_chain.add()
    out_z = out_chain.start(arrived)
    small = sum_over(tie([small], arrived)[0], [("seq", bit) for bit in seq_bits]).reshape(-1)

    blocks = 2 ** len(grad_order(False))
    narrow, broad = width // blocks, hidden_cols // blocks
    keep, got = feed_chain.last()
    gate_out, up_out, down_out = finish_rows(
        core,
        keep,
        got,
        [broad] + [narrow] * cutting + [broad] + [narrow] * (tiles - cutting),
        [
            ([1 + j for j in range(cutting)] + [2 + j for j in range(cutting, tiles)], False),
            ([0, 1 + cutting], True),
        ],
    )
    keep, got = out_chain.last()
    cross_out_out, cross_query_out, self_out_out = finish_rows(
        core, keep, got, [narrow] * 6, [([0, 3], True), ([1, 4], True), ([2, 5], True)]
    )
    keep, got = in_chain.last()
    cross_key_out, cross_value_out, self_query_out, self_key_out, self_value_out = finish_rows(
        core, keep, got, [narrow] * 6, [([0, 3], False), ([1, 4], True), ([2, 5], False)]
    )

    return (
        unflat(outputs),
        unflat(input_grad),
        unflat(memory_grad),
        small[:width],
        self_query_out,
        self_key_out,
        self_value_out,
        self_out_out,
        small[3 * width :].reshape(buckets, -1),
        small[width : 2 * width],
        cross_query_out,
        cross_key_out,
        cross_value_out,
        cross_out_out,
        small[2 * width : 3 * width],
        gate_out,
        up_out,
        down_out,
    )


def solution(mesh):
    placed = P("seq", "dp", None)
    rows = P(("dp", "seq"), None)
    return jax.shard_map(
        per_device,
        mesh=mesh,
        in_specs=(placed, placed, P("dp"), P("dp")) + (P(),) * 16 + (placed,),
        out_specs=(
            placed,
            placed,
            placed,
            P(),
            rows,
            rows,
            rows,
            rows,
            P(),
            P(),
            rows,
            rows,
            rows,
            rows,
            P(),
            rows,
            rows,
            rows,
        ),
        check_vma=False,
    )
```
